128 devices in a mesh: img: 8 (over z_lo, x), cls: 16 (over z_hi, y, core).
Axes of the slice: x: 4, y: 4, z: 4 (z_hi: 2, z_lo: 2; z = z_hi * 2 + z_lo), core: 2. Of those that a mesh axis runs over, the one named last changes fastest.
Arguments:
- spectra: bfloat16 [32768, 64, 256], P(('img', 'cls')), may hold values from -40 to 40
- offsets: int32 [32768, 2], P(('img', 'cls')), may hold values from -6 to 6
- groups: int32 [32768], P(('img', 'cls')), may hold values from 0 to 31
- ctf: float32 [32, 64], replicated, may hold values from -1 to 1
- noise_weight: float32 [64], replicated, may hold values from 0.008 to 0.08
- references: bfloat16 [256, 16384], P('cls'), may hold values from -5 to 5
Outputs:
- class_sums: float32 [256, 16384], P('cls', 'img')
- max_prob: float32 [32768], P(('img', 'cls'))
The draws below stay inside these ranges and needn't reach their ends.
All inputs are finite; a program needn't handle non-finite values.
Results may differ from the reference program's by a relative error of at most 0.019.
Values may be sent and summed in bfloat16 or wider, within the bound.
A program may use at most 128 MiB of HBM per device.

```python
import math
import jax
import jax.numpy as jnp
from jax import lax

IMG_DEV = 256
R = 64
A = 128
ROTS = 16
GROUPS = 32
IMAGES = 32768
CLASSES = 256


def shared_tables(key):
    ref_key = jax.random.fold_in(key, 101)
    ctf_key = jax.random.fold_in(key, 102)
    weight_key = jax.random.fold_in(key, 103)
    group_key = jax.random.fold_in(key, 104)
    shift_key = jax.random.fold_in(key, 105)
    references = jnp.clip(jax.random.normal(ref_key, (CLASSES, 2 * R * A), jnp.float32), -5.0, 5.0)
    ctf = jax.random.uniform(ctf_key, (GROUPS, R), jnp.float32, -1.0, 1.0)
    lowest = math.log(0.008)
    highest = math.log(0.08)
    noise_weight = jnp.exp(jax.random.uniform(weight_key, (R,), jnp.float32, lowest, highest))
    groups = jax.random.randint(group_key, (IMAGES,), 0, GROUPS, jnp.int32)
    offsets = jax.random.randint(shift_key, (IMAGES, 2), -6, 7, jnp.int32)
    return (references, ctf, noise_weight, groups, offsets)


def drawn_rows(key, references, ctf, noise_weight, groups, offsets, picked, levels):
    count = picked.shape[0]
    class_key = jax.random.fold_in(key, 11)
    turn_key = jax.random.fold_in(key, 12)
    level_key = jax.random.fold_in(key, 13)
    chosen_class = jax.random.randint(class_key, (count,), 0, CLASSES, jnp.int32)
    first_turn = jax.random.randint(turn_key, (count,), 0, ROTS, jnp.int32)
    second_turn = (first_turn + ROTS // 2) % ROTS
    level_table = jnp.asarray(levels, jnp.float32)
    strength = level_table[jax.random.randint(level_key, (count,), 0, len(levels), jnp.int32)]
    ordered = references.reshape(CLASSES, ROTS, 2, R, A // ROTS).transpose(0, 2, 3, 4, 1).reshape(CLASSES, 2, R, A)
    chosen = ordered[chosen_class]
    contrast = ctf[groups[picked]]
    energy = jnp.sum(chosen * chosen, axis=(1, 3))
    power = jnp.sum(noise_weight[None, :] * contrast * contrast * energy, axis=1)
    first_scale = 0.5 + strength
    second_scale = first_scale - jnp.minimum(2.0 / jnp.maximum(power, 0.001), 1.0)
    orders = jnp.arange(A, dtype=jnp.int32)
    first_angle = 2.0 * math.pi * (orders[None, :] * first_turn[:, None] % ROTS).astype(jnp.float32) / ROTS
    second_angle = 2.0 * math.pi * (orders[None, :] * second_turn[:, None] % ROTS).astype(jnp.float32) / ROTS
    coef_re = first_scale[:, None] * jnp.cos(first_angle) + second_scale[:, None] * jnp.cos(second_angle)
    coef_im = -(first_scale[:, None] * jnp.sin(first_angle) + second_scale[:, None] * jnp.sin(second_angle))
    target_re = chosen[:, 0] * coef_re[:, None, :] - chosen[:, 1] * coef_im[:, None, :]
    target_im = chosen[:, 0] * coef_im[:, None, :] + chosen[:, 1] * coef_re[:, None, :]
    samples = jnp.arange(A, dtype=jnp.int32)
    spin = 2.0 * math.pi * (orders[:, None] * samples[None, :] % A).astype(jnp.float32) / A
    cos_table = jnp.cos(spin) / math.sqrt(A)
    sin_table = jnp.sin(spin) / math.sqrt(A)
    highest = lax.Precision.HIGHEST
    wave_re = jnp.einsum('nrm,ma->nra', target_re, cos_table, precision=highest) - jnp.einsum('nrm,ma->nra', target_im, sin_table, precision=highest)
    wave_im = jnp.einsum('nrm,ma->nra', target_re, sin_table, precision=highest) + jnp.einsum('nrm,ma->nra', target_im, cos_table, precision=highest)
    theta = 2.0 * math.pi * jnp.arange(A, dtype=jnp.float32) / A
    radius = jnp.arange(R, dtype=jnp.float32) + 1.0
    shifts = offsets[picked].astype(jnp.float32)
    along = jnp.cos(theta)[None, None, :] * shifts[:, 0, None, None] + jnp.sin(theta)[None, None, :] * shifts[:, 1, None, None]
    phase = -2.0 * math.pi * radius[None, :, None] * along / (2.0 * R)
    cosine = jnp.cos(phase)
    sine = jnp.sin(phase)
    out_re = contrast[:, :, None] * (wave_re * cosine + wave_im * sine)
    out_im = contrast[:, :, None] * (wave_im * cosine - wave_re * sine)
    return jnp.clip(jnp.concatenate([out_re, out_im], axis=-1), -40.0, 40.0)


def draw_spectra(key, part):
    references, ctf, noise_weight, groups, offsets = shared_tables(key)
    key = jax.random.fold_in(key, 7)
    every = 32
    blocks = IMAGES // every
    slot_key = jax.random.fold_in(key, 1)
    noise_key = jax.random.fold_in(key, 2)
    plant_key = jax.random.fold_in(key, 3)
    slot = jax.random.randint(slot_key, (blocks,), 0, every, jnp.int32)
    picked = jnp.arange(blocks, dtype=jnp.int32) * every + slot
    noise = jnp.clip(jax.random.normal(noise_key, (blocks, every, R, 2 * A), jnp.float32), -6.0, 6.0)
    noise = noise.astype(jnp.bfloat16)
    planted = drawn_rows(plant_key, references, ctf, noise_weight, groups, offsets, picked, (1.0, 1.5, 2.5)).astype(jnp.bfloat16)
    marker = jnp.arange(every, dtype=jnp.int32)[None, :] == slot[:, None]
    merged = jnp.where(marker[:, :, None, None], planted[:, None, :, :], noise)
    return merged.reshape(IMAGES, R, 2 * A)


def draw_offsets(key, part):
    references, ctf, noise_weight, groups, offsets = shared_tables(key)
    return offsets


def draw_groups(key, part):
    references, ctf, noise_weight, groups, offsets = shared_tables(key)
    return groups


def draw_ctf(key, part):
    references, ctf, noise_weight, groups, offsets = shared_tables(key)
    return ctf


def draw_noise_weight(key, part):
    references, ctf, noise_weight, groups, offsets = shared_tables(key)
    return noise_weight


def draw_references(key, part):
    references, ctf, noise_weight, groups, offsets = shared_tables(key)
    return references.astype(jnp.bfloat16)


def setup_inputs(seed: int = 0) -> dict:
    streams_of = jax.random.split(jax.random.key(seed), 7)
    return {
        "spectra": draw_spectra(jax.random.fold_in(streams_of[6], 71), 0),
        "offsets": draw_offsets(jax.random.fold_in(streams_of[6], 71), 0),
        "groups": draw_groups(jax.random.fold_in(streams_of[6], 71), 0),
        "ctf": draw_ctf(jax.random.fold_in(streams_of[6], 71), 0),
        "noise_weight": draw_noise_weight(jax.random.fold_in(streams_of[6], 71), 0),
        "references": draw_references(jax.random.fold_in(streams_of[6], 71), 0),
    }


def rotation_table():
    idx = jnp.arange(ROTS, dtype=jnp.float32)
    angle = 2.0 * math.pi * idx[:, None] * idx[None, :] / ROTS
    return jnp.stack([jnp.cos(angle), jnp.sin(angle)], axis=0)

def back_table():
    idx = jnp.arange(ROTS, dtype=jnp.float32)
    angle = 2.0 * math.pi * idx[:, None] * idx[None, :] / ROTS
    return jnp.stack([jnp.cos(angle), jnp.sin(angle)], axis=1)

def harmonic_table(angles):
    quarter = angles // ROTS
    samples = jnp.arange(angles, dtype=jnp.int32)
    orders = ROTS * jnp.arange(quarter, dtype=jnp.int32)[None, :] + jnp.arange(ROTS, dtype=jnp.int32)[:, None]
    turns = samples[:, None, None] * orders[None, :, :] % angles
    angle = 2.0 * math.pi * turns.astype(jnp.float32) / angles
    cosine = jnp.cos(angle)
    sine = jnp.sin(angle)
    upper = jnp.stack([cosine, -sine], axis=2)
    lower = jnp.stack([sine, cosine], axis=2)
    return jnp.concatenate([upper, lower], axis=0) / math.sqrt(angles)

def prepare(spectra, offsets, groups, ctf, noise_weight):
    count, cycles, double = spectra.shape
    angles = double // 2
    values = spectra.astype(jnp.float32)
    real_part = values[:, :, :angles]
    imag_part = values[:, :, angles:]
    theta = 2.0 * math.pi * jnp.arange(angles, dtype=jnp.float32) / angles
    radius = jnp.arange(cycles, dtype=jnp.float32) + 1.0
    shift_x = offsets[:, 0].astype(jnp.float32)
    shift_y = offsets[:, 1].astype(jnp.float32)
    along = jnp.cos(theta)[None, None, :] * shift_x[:, None, None] + jnp.sin(theta)[None, None, :] * shift_y[:, None, None]
    phase = -2.0 * math.pi * radius[None, :, None] * along / (2.0 * cycles)
    onehot = (groups[:, None] == jnp.arange(ctf.shape[0], dtype=jnp.int32)[None, :]).astype(jnp.float32)
    contrast = jnp.dot(onehot, ctf, precision=lax.Precision.HIGHEST)
    cosine = jnp.cos(phase)
    sine = jnp.sin(phase)
    shifted_re = contrast[:, :, None] * (real_part * cosine - imag_part * sine)
    shifted_im = contrast[:, :, None] * (real_part * sine + imag_part * cosine)
    merged = jnp.concatenate([shifted_re, shifted_im], axis=-1)
    harm = jnp.einsum('nrc,cjpq->njprq', merged, harmonic_table(angles), precision=lax.Precision.HIGHEST)
    harm = harm.astype(jnp.bfloat16).reshape(count, ROTS, 2 * cycles * (angles // ROTS))
    weights = noise_weight[None, :] * contrast * contrast
    return (harm, weights)

def block_scores(harm, refs, weights, noise_weight):
    count = harm.shape[0]
    blocks = refs.shape[0]
    cycles = weights.shape[1]
    inner = refs.shape[1] // (2 * ROTS)
    raw = refs.astype(jnp.float32).reshape(blocks, ROTS, 2, cycles, inner // cycles)
    energy = lax.optimization_barrier(jnp.sum(raw * raw, axis=(1, 2, 4)))
    refw = (raw * noise_weight[None, None, None, :, None]).astype(jnp.bfloat16).reshape(blocks, ROTS, 2, inner)
    real_ref = refw[:, :, 0]
    imag_ref = refw[:, :, 1]
    pair = jnp.stack([jnp.concatenate([real_ref, imag_ref], -1), jnp.concatenate([imag_ref, -real_ref], -1)], axis=2)
    corr = jnp.einsum('njk,cjok->ncoj', harm.astype(jnp.float32), pair.astype(jnp.float32), precision=lax.Precision.HIGHEST)
    cross = jnp.einsum('ncoj,ojk->nck', corr, rotation_table(), precision=lax.Precision.HIGHEST)
    normt = jnp.dot(weights, energy.T, precision=lax.Precision.HIGHEST)
    return (cross - 0.5 * normt[:, :, None]).reshape(count, blocks * ROTS)

def block_sums(wblock, harm):
    count = harm.shape[0]
    blocks = wblock.shape[1]
    inner = harm.shape[2] // 2
    stacked = harm.reshape(count, ROTS, 2, inner).astype(jnp.float32)
    out = jnp.einsum('ncwj,njhk->cjwhk', wblock.astype(jnp.float32), stacked, precision=lax.Precision.HIGHEST)
    real_sum = out[:, :, 0, 0] - out[:, :, 1, 1]
    imag_sum = out[:, :, 0, 1] + out[:, :, 1, 0]
    return jnp.stack([real_sum, imag_sum], axis=2).reshape(blocks, ROTS * 2 * inner)

def reference(spectra, offsets, groups, ctf, noise_weight, references):
    blocks = IMAGES // IMG_DEV
    spec_b = spectra.reshape(blocks, IMG_DEV, spectra.shape[1], spectra.shape[2])
    off_b = offsets.reshape(blocks, IMG_DEV, 2)
    grp_b = groups.reshape(blocks, IMG_DEV)
    classes = references.shape[0]

    def step(total, items):
        spec, off, grp = items
        harm, weights = prepare(spec, off, grp, ctf, noise_weight)
        scores = block_scores(harm, references, weights, noise_weight)
        top = lax.optimization_barrier(jnp.max(scores, axis=-1, keepdims=True))
        expo = jnp.exp(scores - top)
        prob = expo / lax.optimization_barrier(jnp.sum(expo, axis=-1, keepdims=True))
        best = lax.optimization_barrier(jnp.max(prob, axis=-1))
        wt = jnp.einsum('nck,kwj->ncwj', prob.reshape(IMG_DEV, classes, ROTS), back_table(), precision=lax.Precision.HIGHEST)
        wt = wt.astype(jnp.bfloat16)
        partial_term = block_sums(wt, harm).astype(jnp.bfloat16)
        partial_term = lax.optimization_barrier(partial_term)
        return (total + partial_term.astype(jnp.float32), best)
    start = jnp.zeros((classes, references.shape[1]), jnp.float32)
    class_sums, best = lax.scan(step, start, (spec_b, off_b, grp_b))
    return (class_sums, best.reshape(IMAGES))
```

```python
import math

import jax
import jax.numpy as jnp
import ml_dtypes
import numpy as np
from jax import lax
from jax.experimental import pallas as pl
from jax.experimental.pallas import tpu as pltpu
from jax.sharding import PartitionSpec as P

MESH = pl.DeviceIdType.MESH
F32 = jnp.float32
BF16 = jnp.bfloat16
HIGHEST = lax.Precision.HIGHEST

IMG = 256
R = 64
A = 128
ROTS = 16
SHIFTS = 13
LOW = 192
DEPTH = 384
WX, WY, WZ = 384, 256, 384

S1 = math.sqrt(0.5)
C1 = math.cos(math.pi / 8)
C3 = math.cos(3 * math.pi / 8)


def split_np(values):
    high = values.astype(np.float32).astype(ml_dtypes.bfloat16)
    low = (values - high.astype(np.float64)).astype(np.float32).astype(ml_dtypes.bfloat16)
    return high, low


def shift_table():
    theta = 2.0 * np.pi * np.arange(A) / A
    radius = np.arange(R) + 1.0
    step = np.arange(SHIFTS) - 6.0
    along = (
        np.cos(theta)[None, None, :] * step[:, None, None]
        + np.sin(theta)[None, None, :] * step[None, :, None]
    ).reshape(SHIFTS * SHIFTS, A)
    phase = -2.0 * np.pi * radius[:, None, None] * along[None] / (2.0 * R)
    both = np.concatenate([np.cos(phase), np.sin(phase)], axis=-1)
    high, low = split_np(both)
    table = np.zeros((R, DEPTH, 2 * A), ml_dtypes.bfloat16)
    table[:, : SHIFTS * SHIFTS] = high
    table[:, LOW : LOW + SHIFTS * SHIFTS] = low
    return table


def harmonic_rows():
    quarter = A // ROTS
    orders = ROTS * np.arange(quarter)[None, :] + np.arange(ROTS)[:, None]
    turns = (np.arange(A)[:, None, None] * orders[None]) % A
    angle = 2.0 * np.pi * turns / A
    upper = np.stack([np.cos(angle), -np.sin(angle)], axis=2)
    lower = np.stack([np.sin(angle), np.cos(angle)], axis=2)
    table = np.concatenate([upper, lower], axis=0) / math.sqrt(A)
    rows = np.ascontiguousarray(table.reshape(2 * A, 2 * A).T)
    high, low = split_np(rows)
    return np.concatenate([high, low, high], axis=1)


def cosine_part(a):
    p, m = a[0] + a[8], a[0] - a[8]
    t, d = a[2] + a[6], S1 * (a[2] - a[6])
    q = p + a[4]
    even = [q + t, m + d, p - a[4], m - d, q - t]
    s17, d17 = a[1] + a[7], a[1] - a[7]
    s35, d35 = a[3] + a[5], a[3] - a[5]
    odd = [s17 + s35, C1 * d17 + C3 * d35, S1 * (s17 - s35), C3 * d17 - C1 * d35]
    out = [even[k] + odd[k] for k in range(4)] + [even[4]]
    return out + [even[k] - odd[k] for k in (3, 2, 1, 0)]


def sine_part(b):
    t = S1 * (b[2] + b[6])
    even = [None, t + b[4], b[2] - b[6], t - b[4]]
    s17, d17 = b[1] + b[7], b[1] - b[7]
    s35, d35 = b[3] + b[5], b[3] - b[5]
    odd = [None, C3 * s17 + C1 * s35, S1 * (d17 + d35), C1 * s17 - C3 * s35, d17 - d35]
    out = [None] + [odd[k] + even[k] for k in (1, 2, 3)] + [odd[4]]
    return out + [odd[k] - even[k] for k in (3, 2, 1)]


def across(a, b, precision=None):
    return lax.dot_general(
        a, b, (((1,), (1,)), ((), ())), precision=precision, preferred_element_type=F32
    )


def plain(a, b, precision=None):
    return jnp.dot(a, b, precision=precision, preferred_element_type=F32)


def kernel(
    spectra, table, offsets, groups, ctf, noise, refs, harmonics,
    sums_out, prob_out,
    gx, gy, gz, cx, cy, cz, ht, qb, wb, norm, spec, tab, hot, cgt,
    rx1, ry1, rz1, rx2, ry2, rz2, rx3, ry3, rz3,
    dma, ag_s, ag_r, core_s, core_r, x1_s, x1_r, y1_s, y1_r, z1_s, z1_r, late_s, late_r,
):
    img = lax.axis_index("img")
    cls = lax.axis_index("cls")
    zl, x = img // 4, img % 4
    zh, y, e = cls // 8, (cls // 2) % 4, cls % 2
    other = 1 - e

    def device(zl_, x_, zh_, y_, e_):
        return (zl_ * 4 + x_, zh_ * 8 + y_ * 2 + e_)

    def at_x(d):
        return device(zl, (x + d) % 4, zh, y, e)

    def at_y(d):
        return device(zl, x, zh, (y + d) % 4, e)

    def flip(d):
        return (zh + d // 2) % 2, (zl + d) % 2

    def at_z(d):
        zh_, zl_ = flip(d)
        return device(zl_, x, zh_, y, e)

    def at_zy(d):
        return device((zl + 1) % 2, x, (zh + 1) % 2, (y + d) % 4, e)

    twin = device(zl, x, zh, y, other)

    def remote(src, dst, send, recv, where):
        return pltpu.make_async_remote_copy(
            src_ref=src, dst_ref=dst, send_sem=send, recv_sem=recv,
            device_id=where, device_id_type=MESH,
        )

    def spec_copy(c):
        return pltpu.make_async_copy(
            spectra.at[:, pl.ds(c * 16, 16), :], spec.at[c % 2], dma.at[c % 2]
        )

    def tab_copy(c):
        return pltpu.make_async_copy(
            table.at[pl.ds(c * 16, 16)], tab.at[c % 2], dma.at[2 + c % 2]
        )

    spec_copy(0).start()
    tab_copy(0).start()

    barrier = pltpu.get_barrier_semaphore()
    friends = [twin]
    friends += [at_x(d) for d in (1, 2, 3)]
    friends += [at_y(d) for d in (1, 2, 3)]
    friends += [at_z(d) for d in (1, 2, 3)]
    friends += [at_zy(d) for d in (1, 2, 3)]
    for friend in friends:
        pl.semaphore_signal(barrier, inc=1, device_id=friend, device_id_type=MESH)

    spread = (
        lax.broadcasted_iota(jnp.int32, (R, 512), 0)
        == lax.broadcasted_iota(jnp.int32, (R, 512), 1) // 8
    ).astype(F32)
    nw = jnp.broadcast_to(noise[...], (8, R))
    nwx = plain(nw, spread, HIGHEST)[0:1]

    def weighted(start, width, gains):
        part = refs[:, pl.ds(pl.multiple_of(start, 128), width)].astype(F32)
        return (part * gains).astype(BF16)

    gain_x = nwx[:, :384]
    gain_y = jnp.concatenate([nwx[:, 384:], nwx[:, :128]], axis=1)
    gain_z = nwx[:, 128:]
    for k in range(4):
        j = (k // 2) * 8 + x * 2 + k % 2
        gx[e, zh, y, x, k] = weighted(j * 1024, WX, gain_x)
    for k in range(8):
        j = zl * 8 + k
        gz[e, zh, y, zl, k] = weighted(j * 1024 + WX + WY, WZ, gain_z)
    for j in range(16):
        gy[e, zh, y, j] = weighted(j * 1024 + WX, WY, gain_y)
    total = jnp.zeros((16, 512), F32)
    for k in range(32):
        part = refs[:, k * 512 : (k + 1) * 512].astype(F32)
        total = total + part * part
    ctf4 = jnp.concatenate([ctf[...]] * 4, axis=0)
    by_group = plain(0.5 * noise[...] * ctf4 * ctf4, spread, HIGHEST)
    energy = across(total, by_group, HIGHEST)
    high = energy.astype(BF16).astype(F32)
    middle = (energy - high).astype(BF16).astype(F32)
    low = energy - high - middle
    lane = lax.broadcasted_iota(jnp.int32, (16, 128), 1) // 32
    packed = jnp.where(
        lane == 0, high, jnp.where(lane == 1, middle, jnp.where(lane == 2, low, 0.0))
    ).astype(BF16)
    gy[e, zh, y, 16] = jnp.concatenate([packed, packed], axis=1)

    def ag(index, piece, where):
        return remote(piece, piece, ag_s.at[index], ag_r.at[index], where)

    mine_x = gx.at[e, zh, y, x]
    pre_x = [ag(d - 1, mine_x, at_y(d)) for d in (1, 2, 3)]
    pre_x += [ag(3, mine_x, at_z(3))]
    pre_x += [ag(3 + d, mine_x, at_zy(d)) for d in (1, 2, 3)]
    pre_z = [ag(6 + d, gz.at[e, zh, y, zl], at_y(d)) for d in (1, 2, 3)]
    pre_y = [ag(10, gy.at[e, zh, y], at_z(3))]
    last_x = [ag(10 + d, gx.at[e, :, :, x], at_x(d)) for d in (1, 2, 3)]
    last_y = [ag(13 + d, gy.at[e, :, y], at_y(d)) for d in (1, 2, 3)]
    last_z = [ag(16 + d, gz.at[e, zh, :, zl], at_z(d)) for d in (1, 2, 3)]

    def piece_x(e_, d):
        return gx.at[e_, :, :, (x + d) % 4]

    def piece_y(e_, d):
        return gy.at[e_, :, (y + d) % 4]

    def piece_z(e_, d):
        zh_, zl_ = flip(d)
        return gz.at[e_, zh_, :, zl_]

    pieces = (piece_x, piece_y, piece_z)

    def share(group, d):
        return ag(20 + 4 * group + d, pieces[group](e, d), twin)

    pl.semaphore_wait(barrier, len(friends))
    for copy in pre_x + pre_y + pre_z:
        copy.start()

    index = (offsets[:, 0:1] + 6) * SHIFTS + offsets[:, 1:2] + 6
    column = lax.broadcasted_iota(jnp.int32, (IMG, DEPTH), 1)
    hot[...] = ((column == index) | (column == index + LOW)).astype(F32).astype(BF16)
    of_group = (
        lax.broadcasted_iota(jnp.int32, (32, IMG), 0) == groups[...]
    ).astype(F32)
    cgt[...] = lax.dot_general(
        ctf[...], of_group, (((0,), (0,)), ((), ())), precision=HIGHEST, preferred_element_type=F32
    )

    def prepare(c):
        slot = c % 2
        if c < 3:
            spec_copy(c + 1).start()
            tab_copy(c + 1).start()
        spec_copy(c).wait()
        tab_copy(c).wait()

        @pl.loop(0, 16)
        def widen(b):
            part = spec[slot, pl.ds(b * 16, 16)].astype(F32)
            rows = pl.ds(pl.multiple_of(b * 256, 256), 256)
            qb[rows, :] = part[:, :, :A].reshape(256, A)
            rows = pl.ds(pl.multiple_of(4096 + b * 256, 256), 256)
            qb[rows, :] = part[:, :, A:].reshape(256, A)

        @pl.loop(0, 8)
        def pairs(b):
            found = []
            for k in range(2):
                r = b * 2 + k
                turn = plain(hot[...], tab[slot, r])
                cosine, sine = turn[:, :A], turn[:, A:]
                real = qb[pl.ds(r, IMG, stride=16), :]
                imag = qb[pl.ds(4096 + r, IMG, stride=16), :]
                value = jnp.concatenate(
                    [real * cosine - imag * sine, real * sine + imag * cosine], axis=1
                )
                high = value.astype(BF16)
                low = (value - high.astype(F32)).astype(BF16)
                out = across(harmonics[...], jnp.concatenate([high, high, low], axis=1))
                out = out * cgt[pl.ds(c * 16 + r, 1), :]
                found.append(out.reshape(32, 8, IMG))
            both = jnp.concatenate(found, axis=1)
            ht[:, pl.ds(pl.multiple_of(c * 128 + b * 16, 16), 16), :] = both.astype(BF16)

    prepare(0)
    for copy in pre_x:
        copy.wait_recv()
    for copy in last_x:
        copy.start()
    for copy in pre_y + pre_z:
        copy.wait_recv()
    for copy in last_z + last_y:
        copy.start()
    for group in range(3):
        share(group, 0).start()
    prepare(1)
    prepare(2)
    prepare(3)
    for d in (1, 3, 2):
        for group, last in ((1, last_y), (0, last_x), (2, last_z)):
            last[d - 1].wait_recv()
            share(group, d if group == 2 else 4 - d).start()
    for group in range(3):
        for d in range(4):
            share(group, d).wait_recv()

    @pl.loop(0, 16)
    def correlate(j):
        jx = (j // 2) % 4
        jz = j // 8
        part_x = gx[:, :, :, jx, jz * 2 + j % 2].reshape(256, WX)
        part_y = gy[:, :, :, j].reshape(256, WY)
        part_z = gz[:, :, :, jz, j % 8].reshape(256, WZ)
        real = jnp.concatenate([part_x, part_y[:, :128]], axis=1)
        imag = jnp.concatenate([part_y[:, 128:], part_z], axis=1)
        h_re, h_im = ht[2 * j], ht[2 * j + 1]
        q_re = plain(real, h_re) + plain(imag, h_im)
        q_im = plain(imag, h_re) - plain(real, h_im)
        for t in range(2):
            base = pl.multiple_of((t * 32 + 2 * j) * 256, 256)
            qb[pl.ds(base, 256), :] = q_re[:, t * 128 : (t + 1) * 128]
            qb[pl.ds(base + 256, 256), :] = q_im[:, t * 128 : (t + 1) * 128]

    row = lax.broadcasted_iota(jnp.int32, (128, IMG), 0)
    thrice = ((row % 32 == groups[...]) & (row < 96)).astype(F32).astype(BF16)
    norms = plain(gy[:, :, :, 16].reshape(256, WY)[:, :128], thrice)
    norm[0:256, :] = norms[:, :128]
    norm[256:512, :] = norms[:, 128:]

    for t in range(2):
        def at(k, c, t=t):
            return (t * 32 + k) * 256 + c

        def scores(b, top, t=t, at=at):
            c = pl.multiple_of(b * 8, 8)
            re = [qb[pl.ds(at(2 * j, c), 8), :] for j in range(16)]
            im = [qb[pl.ds(at(2 * j + 1, c), 8), :] for j in range(16)]
            a = [re[0]] + [re[j] + re[16 - j] for j in range(1, 8)] + [re[8]]
            s = [None] + [im[j] - im[16 - j] for j in range(1, 8)]
            a[0] = a[0] - norm[pl.ds(t * 256 + c, 8), :]
            cp, sp = cosine_part(a), sine_part(s)
            out = [cp[0]] + [cp[k] + sp[k] for k in range(1, 8)] + [cp[8]]
            out += [cp[16 - k] - sp[16 - k] for k in range(9, 16)]
            for k in range(16):
                qb[pl.ds(at(k, c), 8), :] = out[k]
                top = jnp.maximum(top, out[k])
            return top

        top = lax.fori_loop(0, 32, scores, jnp.full((8, 128), -jnp.inf, F32))
        top = jnp.max(top, axis=0, keepdims=True)

        def exponents(b, total, top=top, at=at):
            c = pl.multiple_of(b * 8, 8)
            for k in range(16):
                value = jnp.exp(qb[pl.ds(at(k, c), 8), :] - top)
                qb[pl.ds(at(k, c), 8), :] = value
                total = total + value
            return total

        total = lax.fori_loop(0, 32, exponents, jnp.zeros((8, 128), F32))
        scale = 1.0 / jnp.sum(total, axis=0, keepdims=True)
        prob_out[:, t * 128 : (t + 1) * 128] = scale

        @pl.loop(0, 16)
        def back(b, t=t, at=at, scale=scale):
            c = pl.multiple_of(b * 16, 16)
            p = [qb[pl.ds(at(k, c), 16), :] * scale for k in range(16)]
            a = [p[0]] + [p[k] + p[16 - k] for k in range(1, 8)] + [p[8]]
            s = [None] + [p[k] - p[16 - k] for k in range(1, 8)]
            cp, sp = cosine_part(a), sine_part(s)
            cols = slice(t * 128, (t + 1) * 128)
            zero = jnp.zeros((16, 128), BF16)
            for j in range(9):
                re = cp[j].astype(BF16)
                wb[j, 0, pl.ds(c, 16), cols] = re
                if j in (0, 8):
                    wb[j, 1, pl.ds(c, 16), cols] = zero
                else:
                    wb[16 - j, 0, pl.ds(c, 16), cols] = re
                    wb[j, 1, pl.ds(c, 16), cols] = sp[j].astype(BF16)
                    wb[16 - j, 1, pl.ds(c, 16), cols] = (-sp[j]).astype(BF16)

    for copy in pre_x + pre_y + pre_z + last_x + last_y + last_z:
        copy.wait_send()
    for group in range(3):
        for d in range(4):
            share(group, d).wait_send()

    def target(it):
        return (x + 1 + it) % 4, (zl + 1 + it // 4) % 2

    def trade(it):
        xt, zt = target(it)
        pairs = (
            (gx.at[other, :, :, xt, pl.ds(zt * 2, 2)], cx.at[:, :, xt, pl.ds(zt * 2, 2)]),
            (gy.at[other, :, :, pl.ds(zt * 8 + xt * 2, 2)], cy.at[:, :, pl.ds(zt * 8 + xt * 2, 2)]),
            (gz.at[other, :, :, zt, pl.ds(xt * 2, 2)], cz.at[:, :, zt, pl.ds(xt * 2, 2)]),
        )
        return [
            remote(src, dst, core_s.at[k, it], core_r.at[k, it], twin)
            for k, (src, dst) in enumerate(pairs)
        ]

    def first_x(it):
        xt, zt = target(it)
        u, half = it % 4, it // 4
        return remote(
            gx.at[e, :, :, xt, pl.ds(zt * 2, 2)], rx1.at[u, zt],
            x1_s.at[u, half], x1_r.at[u, half], at_x(u + 1),
        )

    def first_y(it, d):
        xt, zt = target(it)
        return remote(
            gy.at[e, :, (y + d) % 4, pl.ds(zt * 8 + xt * 2, 2)],
            ry1.at[d - 1, :, pl.ds(zt * 8 + xt * 2, 2)],
            y1_s.at[d - 1, it], y1_r.at[d - 1, it], at_y(d),
        )

    def first_z(it, d):
        xt, zt = target(it)
        u = it % 4
        zh_, zl_ = flip(d)
        return remote(
            gz.at[e, zh_, :, zt, pl.ds(xt * 2, 2)], rz1.at[d - 1, :, pl.ds(xt * 2, 2)],
            z1_s.at[d - 1, u], z1_r.at[d - 1, u], at_z(d),
        )

    def settle(it):
        xt, zt = target(it)
        for copy in trade(it):
            copy.wait_recv()

        @pl.loop(0, 8)
        def add(s):
            h, v = s // 4, s % 4
            k = pl.ds(zt * 2, 2)
            gx[e, h, v, xt, k] = (
                gx[e, h, v, xt, k].astype(F32) + cx[h, v, xt, k].astype(F32)
            ).astype(BF16)
            k = pl.ds(zt * 8 + xt * 2, 2)
            gy[e, h, v, k] = (
                gy[e, h, v, k].astype(F32) + cy[h, v, k].astype(F32)
            ).astype(BF16)
            k = pl.ds(xt * 2, 2)
            gz[e, h, v, zt, k] = (
                gz[e, h, v, zt, k].astype(F32) + cz[h, v, zt, k].astype(F32)
            ).astype(BF16)

        @pl.when(it % 4 != 3)
        def _():
            first_x(it).start()

        @pl.when(it < 4)
        def _():
            first_z(it, 1).start()
            first_z(it, 3).start()

        @pl.when(it >= 4)
        def _():
            first_z(it, 2).start()

        for d in (1, 3, 2):
            first_y(it, d).start()

    @pl.loop(0, 8)
    def accumulate(it):
        xt, zt = target(it)
        for k in range(2):
            j = zt * 8 + xt * 2 + k
            w_re, w_im = wb[j, 0], wb[j, 1]
            w_minus = wb[(16 - j) % 16, 1]
            h_both = jnp.concatenate([ht[2 * j], ht[2 * j + 1]], axis=1)
            out_re = across(jnp.concatenate([w_re, w_minus], axis=1), h_both).astype(BF16)
            out_im = across(jnp.concatenate([w_im, w_re], axis=1), h_both).astype(BF16)
            gx[:, :, :, xt, zt * 2 + k] = out_re[:, :384].reshape(2, 2, 4, 16, WX)
            gy[:, :, :, j] = jnp.concatenate(
                [out_re[:, 384:], out_im[:, :128]], axis=1
            ).reshape(2, 2, 4, 16, WY)
            gz[:, :, :, zt, xt * 2 + k] = out_im[:, 128:].reshape(2, 2, 4, 16, WZ)
        for copy in trade(it):
            copy.start()

        @pl.when(it > 0)
        def _():
            settle(it - 1)

    settle(7)

    for half in range(2):
        for u in range(3):
            first_x(u + 4 * half).wait_recv()

    @pl.loop(0, 8)
    def add_x1(s):
        h, v = s // 4, s % 4
        acc = gx[e, h, v, x].astype(F32).reshape(2, 2, 16, WX)
        for u in range(3):
            acc = acc + rx1[u, :, h, v].astype(F32)
        gx[e, h, v, x] = acc.reshape(4, 16, WX).astype(BF16)

    def late(stage, group, d, src, dst, where):
        return remote(
            src, dst, late_s.at[stage, group, d - 1], late_r.at[stage, group, d - 1], where
        )

    def second_x(d):
        return late(0, 0, d, gx.at[e, :, (y + d) % 4, x], rx2.at[d - 1], at_y(d))

    def second_y(d):
        zh_, zl_ = flip(d)
        return late(0, 1, d, gy.at[e, zh_, y, pl.ds(zl_ * 8, 8)], ry2.at[d - 1], at_z(d))

    def second_z(d):
        return late(
            0, 2, d, gz.at[e, zh, :, zl, pl.ds(((x + d) % 4) * 2, 2)], rz2.at[d - 1], at_x(d)
        )

    def third_x(d):
        zh_, zl_ = flip(d)
        return late(1, 0, d, gx.at[e, zh_, y, x, pl.ds(zl_ * 2, 2)], rx3.at[d - 1], at_z(d))

    def third_y(d):
        return late(
            1, 1, d, gy.at[e, zh, y, pl.ds(zl * 8 + ((x + d) % 4) * 2, 2)], ry3.at[d - 1], at_x(d)
        )

    def third_z(d):
        return late(
            1, 2, d, gz.at[e, zh, (y + d) % 4, zl, pl.ds(x * 2, 2)], rz3.at[d - 1], at_y(d)
        )

    for d in (1, 3, 2):
        second_x(d).start()

    for u in range(4):
        for d in (1, 2, 3):
            first_z(u + (4 if d == 2 else 0), d).wait_recv()

    @pl.loop(0, 4)
    def add_z1(v):
        acc = gz[e, zh, v, zl].astype(F32)
        for d in range(3):
            acc = acc + rz1[d, v].astype(F32)
        gz[e, zh, v, zl] = acc.astype(BF16)

    for d in (1, 3, 2):
        second_z(d).start()

    for it in range(8):
        for d in (1, 2, 3):
            first_y(it, d).wait_recv()

    @pl.loop(0, 8)
    def add_y1(s):
        h, k = s // 4, pl.ds((s % 4) * 4, 4)
        acc = gy[e, h, y, k].astype(F32)
        for d in range(3):
            acc = acc + ry1[d, h, k].astype(F32)
        gy[e, h, y, k] = acc.astype(BF16)

    for d in (1, 3, 2):
        second_y(d).start()

    for d in (1, 3, 2):
        second_x(d).wait_recv()
    for h in range(2):
        acc = gx[e, h, y, x].astype(F32)
        for d in range(3):
            acc = acc + rx2[d, h].astype(F32)
        gx[e, h, y, x] = acc.astype(BF16)
    for d in (1, 3, 2):
        third_x(d).start()

    for d in (1, 3, 2):
        second_z(d).wait_recv()
    k = pl.ds(x * 2, 2)
    for v in range(4):
        acc = gz[e, zh, v, zl, k].astype(F32)
        for d in range(3):
            acc = acc + rz2[d, v].astype(F32)
        gz[e, zh, v, zl, k] = acc.astype(BF16)
    for d in (1, 3, 2):
        third_z(d).start()

    for d in (1, 3, 2):
        second_y(d).wait_recv()
    k = pl.ds(zl * 8, 8)
    acc = gy[e, zh, y, k].astype(F32)
    for d in range(3):
        acc = acc + ry2[d].astype(F32)
    gy[e, zh, y, k] = acc.astype(BF16)
    for d in (1, 3, 2):
        third_y(d).start()

    for third in (third_x, third_z, third_y):
        for d in (1, 2, 3):
            third(d).wait_recv()
    acc_x = gx[e, zh, y, x, pl.ds(zl * 2, 2)].astype(F32)
    acc_y = gy[e, zh, y, pl.ds(zl * 8 + x * 2, 2)].astype(F32)
    acc_z = gz[e, zh, y, zl, pl.ds(x * 2, 2)].astype(F32)
    for d in range(3):
        acc_x = acc_x + rx3[d].astype(F32)
        acc_y = acc_y + ry3[d].astype(F32)
        acc_z = acc_z + rz3[d].astype(F32)
    for k in range(2):
        sums_out[:, k * 1024 : k * 1024 + WX] = acc_x[k]
        sums_out[:, k * 1024 + WX : k * 1024 + WX + WY] = acc_y[k]
        sums_out[:, k * 1024 + WX + WY : (k + 1) * 1024] = acc_z[k]

    for it in range(8):
        for copy in trade(it):
            copy.wait_send()
        if it % 4 != 3:
            first_x(it).wait_send()
        for d in (1, 2, 3):
            first_y(it, d).wait_send()
        for d in (1, 3) if it < 4 else (2,):
            first_z(it, d).wait_send()
    for copy in (second_x, second_y, second_z, third_x, third_y, third_z):
        for d in (1, 2, 3):
            copy(d).wait_send()


def on_device(spectra, offsets, groups, ctf, noise_weight, references):
    vmem = pl.BlockSpec(memory_space=pltpu.VMEM)
    anywhere = pl.BlockSpec(memory_space=pl.ANY)
    sem = pltpu.SemaphoreType.DMA
    sums, prob = pl.pallas_call(
        kernel,
        out_shape=(
            jax.ShapeDtypeStruct((16, 2048), F32),
            jax.ShapeDtypeStruct((1, IMG), F32),
        ),
        in_specs=[anywhere, anywhere] + [vmem] * 6,
        out_specs=(vmem, vmem),
        scratch_shapes=[
            pltpu.VMEM((2, 2, 4, 4, 4, 16, WX), BF16),
            pltpu.VMEM((2, 2, 4, 17, 16, WY), BF16),
            pltpu.VMEM((2, 2, 4, 2, 8, 16, WZ), BF16),
            pltpu.VMEM((2, 4, 4, 4, 16, WX), BF16),
            pltpu.VMEM((2, 4, 16, 16, WY), BF16),
            pltpu.VMEM((2, 4, 2, 8, 16, WZ), BF16),
            pltpu.VMEM((32, 512, IMG), BF16),
            pltpu.VMEM((16384, 128), F32),
            pltpu.VMEM((16, 2, 256, IMG), BF16),
            pltpu.VMEM((512, 128), F32),
            pltpu.VMEM((2, IMG, 16, 2 * A), BF16),
            pltpu.VMEM((2, 16, DEPTH, 2 * A), BF16),
            pltpu.VMEM((IMG, DEPTH), BF16),
            pltpu.VMEM((R, IMG), F32),
            pltpu.VMEM((3, 2, 2, 4, 2, 16, WX), BF16),
            pltpu.VMEM((3, 2, 16, 16, WY), BF16),
            pltpu.VMEM((3, 4, 8, 16, WZ), BF16),
            pltpu.VMEM((3, 2, 4, 16, WX), BF16),
            pltpu.VMEM((3, 8, 16, WY), BF16),
            pltpu.VMEM((3, 4, 2, 16, WZ), BF16),
            pltpu.VMEM((3, 2, 16, WX), BF16),
            pltpu.VMEM((3, 2, 16, WY), BF16),
            pltpu.VMEM((3, 2, 16, WZ), BF16),
            sem((4,)),
            sem((32,)),
            sem((32,)),
            sem((3, 8)),
            sem((3, 8)),
            sem((3, 2)),
            sem((3, 2)),
            sem((3, 8)),
            sem((3, 8)),
            sem((3, 4)),
            sem((3, 4)),
            sem((2, 3, 3)),
            sem((2, 3, 3)),
        ],
        compiler_params=pltpu.CompilerParams(
            collective_id=0, has_side_effects=True, vmem_limit_bytes=60 << 20
        ),
        cost_estimate=pl.CostEstimate(
            flops=14 << 30, bytes_accessed=24 << 20, transcendentals=1 << 20
        ),
        name="classify",
    )(
        spectra,
        jnp.asarray(shift_table()),
        offsets,
        groups.reshape(1, -1),
        ctf,
        noise_weight.reshape(1, -1),
        references,
        jnp.asarray(harmonic_rows()),
    )
    return sums, prob.reshape(-1)


def solution(mesh):
    placed = (
        P(("img", "cls"), None, None),
        P(("img", "cls"), None),
        P(("img", "cls")),
        P(),
        P(),
        P("cls", None),
    )
    return jax.shard_map(
        on_device,
        mesh=mesh,
        in_specs=placed,
        out_specs=(P("cls", "img"), P(("img", "cls"))),
        check_vma=False,
    )
```

```python
import math

import jax
import jax.numpy as jnp
import ml_dtypes
import numpy as np
from jax import lax
from jax.experimental import pallas as pl
from jax.experimental.pallas import tpu as pltpu
from jax.sharding import PartitionSpec as P

MESH = pl.DeviceIdType.MESH
F32 = jnp.float32
BF16 = jnp.bfloat16
HIGHEST = lax.Precision.HIGHEST

IMG = 256
R = 64
A = 128
ROTS = 16
SHIFTS = 13
KINDS = (SHIFTS * SHIFTS + 1) // 2
LOW = 88
DEPTH = 176
WX, WY, WZ = 384, 256, 384

S1 = math.sqrt(0.5)
C1 = math.cos(math.pi / 8)
C3 = math.cos(3 * math.pi / 8)


def split_np(values):
    high = values.astype(np.float32).astype(ml_dtypes.bfloat16)
    low = (values - high.astype(np.float64)).astype(np.float32).astype(ml_dtypes.bfloat16)
    return high, low


def shift_table():
    theta = 2.0 * np.pi * np.arange(A) / A
    radius = np.arange(R) + 1.0
    step = np.arange(SHIFTS) - 6.0
    along = (
        np.cos(theta)[None, None, :] * step[:, None, None]
        + np.sin(theta)[None, None, :] * step[None, :, None]
    ).reshape(SHIFTS * SHIFTS, A)[:KINDS]
    phase = -2.0 * np.pi * radius[:, None, None] * along[None] / (2.0 * R)
    both = np.concatenate([np.cos(phase), np.sin(phase)], axis=-1)
    high, low = split_np(both)
    table = np.zeros((R, DEPTH, 2 * A), ml_dtypes.bfloat16)
    table[:, :KINDS] = high
    table[:, LOW : LOW + KINDS] = low
    return table


def harmonic_rows():
    quarter = A // ROTS
    orders = ROTS * np.arange(quarter)[None, :] + np.arange(ROTS)[:, None]
    turns = (np.arange(A)[:, None, None] * orders[None]) % A
    angle = 2.0 * np.pi * turns / A
    upper = np.stack([np.cos(angle), -np.sin(angle)], axis=2)
    lower = np.stack([np.sin(angle), np.cos(angle)], axis=2)
    table = np.concatenate([upper, lower], axis=0) / math.sqrt(A)
    return np.ascontiguousarray(table.reshape(2 * A, 2 * A).T).astype(np.float32).astype(
        ml_dtypes.bfloat16
    )


def cosine_part(a):
    p, m = a[0] + a[8], a[0] - a[8]
    t, d = a[2] + a[6], S1 * (a[2] - a[6])
    q = p + a[4]
    even = [q + t, m + d, p - a[4], m - d, q - t]
    s17, d17 = a[1] + a[7], a[1] - a[7]
    s35, d35 = a[3] + a[5], a[3] - a[5]
    odd = [s17 + s35, C1 * d17 + C3 * d35, S1 * (s17 - s35), C3 * d17 - C1 * d35]
    out = [even[k] + odd[k] for k in range(4)] + [even[4]]
    return out + [even[k] - odd[k] for k in (3, 2, 1, 0)]


def sine_part(b):
    t = S1 * (b[2] + b[6])
    even = [None, t + b[4], b[2] - b[6], t - b[4]]
    s17, d17 = b[1] + b[7], b[1] - b[7]
    s35, d35 = b[3] + b[5], b[3] - b[5]
    odd = [None, C3 * s17 + C1 * s35, S1 * (d17 + d35), C1 * s17 - C3 * s35, d17 - d35]
    out = [None] + [odd[k] + even[k] for k in (1, 2, 3)] + [odd[4]]
    return out + [odd[k] - even[k] for k in (3, 2, 1)]


def across(a, b, precision=None):
    return lax.dot_general(
        a, b, (((1,), (1,)), ((), ())), precision=precision, preferred_element_type=F32
    )


def plain(a, b, precision=None):
    return jnp.dot(a, b, precision=precision, preferred_element_type=F32)


def kernel(
    spectra, table, offsets, groups, ctf, noise, refs, harmonics,
    sums_out, prob_out,
    gx, gy, gz, gt, cx, cy, cz, ht, qb, wb, norm, spec, tab, moved, hot, sign, cgt,
    rx1, ry1, rz1, rx2, ry2, rz2, rx3, ry3, rz3,
    dma, ag_s, ag_r, core_s, core_r, x1_s, x1_r, y1_s, y1_r, z1_s, z1_r, late_s, late_r,
):
    img = lax.axis_index("img")
    cls = lax.axis_index("cls")
    zl, x = img // 4, img % 4
    zh, y, e = cls // 8, (cls // 2) % 4, cls % 2
    other = 1 - e

    def device(zl_, x_, zh_, y_, e_):
        return (zl_ * 4 + x_, zh_ * 8 + y_ * 2 + e_)

    def at_x(d):
        return device(zl, (x + d) % 4, zh, y, e)

    def at_y(d):
        return device(zl, x, zh, (y + d) % 4, e)

    def flip(d):
        return (zh + d // 2) % 2, (zl + d) % 2

    def at_z(d):
        zh_, zl_ = flip(d)
        return device(zl_, x, zh_, y, e)

    def at_zy(d):
        return device((zl + 1) % 2, x, (zh + 1) % 2, (y + d) % 4, e)

    twin = device(zl, x, zh, y, other)

    def remote(src, dst, send, recv, where):
        return pltpu.make_async_remote_copy(
            src_ref=src, dst_ref=dst, send_sem=send, recv_sem=recv,
            device_id=where, device_id_type=MESH,
        )

    def spec_copy(c):
        return pltpu.make_async_copy(
            spectra.at[:, pl.ds(c * 16, 16), :], spec.at[c % 2], dma.at[c % 2]
        )

    def tab_copy(c):
        return pltpu.make_async_copy(
            table.at[pl.ds(c * 16, 16)], tab.at[c % 2], dma.at[2 + c % 2]
        )

    barrier = pltpu.get_barrier_semaphore()
    friends = [twin]
    friends += [at_x(d) for d in (1, 2, 3)]
    friends += [at_y(d) for d in (1, 2, 3)]
    friends += [at_z(d) for d in (1, 2, 3)]
    friends += [at_zy(d) for d in (1, 2, 3)]
    for friend in friends:
        pl.semaphore_signal(barrier, inc=1, device_id=friend, device_id_type=MESH)
    spec_copy(0).start()
    tab_copy(0).start()

    spread = (
        lax.broadcasted_iota(jnp.int32, (R, 512), 0)
        == lax.broadcasted_iota(jnp.int32, (R, 512), 1) // 8
    ).astype(F32)
    nw = jnp.broadcast_to(noise[...], (8, R))
    nwx = plain(nw, spread, HIGHEST)[0:1]

    def weighted(j, first, width, gains):
        start = j * 1024 + first
        part = refs[:, pl.ds(pl.multiple_of(start, 128), width)].astype(F32)
        return (part * gains).astype(BF16)

    gain_x = nwx[:, :384]
    gain_y = jnp.concatenate([nwx[:, 384:], nwx[:, :128]], axis=1)
    gain_z = nwx[:, 128:]
    for h in range(2):
        for k in range(2):
            gx[e, zh, y, x, h, k] = weighted(k * 8 + x * 2 + h, 0, WX, gain_x)
        for k in range(4):
            gz[e, zh, y, zl, h, k] = weighted(zl * 8 + k * 2 + h, WX + WY, WZ, gain_z)
        for k in range(8):
            gy[e, zh, y, h, k // 2, k % 2] = weighted(
                (k % 2) * 8 + (k // 2) * 2 + h, WX, WY, gain_y
            )

    def ag(h, index, piece, where):
        return remote(piece, piece, ag_s.at[h, index], ag_r.at[h, index], where)

    def pre_x(h):
        mine = gx.at[e, zh, y, x, h]
        out = [ag(h, d - 1, mine, at_y(d)) for d in (1, 3, 2)] + [ag(h, 3, mine, at_z(3))]
        return out + [ag(h, 3 + d, mine, at_zy(d)) for d in (1, 3, 2)]

    def pre_z(h):
        return [ag(h, 6 + d, gz.at[e, zh, y, zl, h], at_y(d)) for d in (1, 3, 2)]

    def pre_y(h):
        return [ag(h, 10, gy.at[e, zh, y, h], at_z(3))]

    pre_t = ag(0, 32, gt.at[e, zh, y], at_z(3))

    def piece_x(h, e_, d):
        return gx.at[e_, :, :, (x + d) % 4, h]

    def piece_y(h, e_, d):
        return gy.at[e_, :, (y + d) % 4, h]

    def piece_z(h, e_, d):
        zh_, zl_ = flip(d)
        return gz.at[e_, zh_, :, zl_, h]

    def last_x(h, d):
        return ag(h, 10 + d, piece_x(h, e, 0), at_x(d))

    def last_y(h, d):
        return ag(h, 13 + d, piece_y(h, e, 0), at_y(d))

    def last_z(h, d):
        return ag(h, 16 + d, piece_z(h, e, 0), at_z(d))

    def last_t(d):
        return ag(0, 32 + d, gt.at[e, :, y], at_y(d))

    pieces = (piece_x, piece_y, piece_z)
    lasts = (last_x, last_y, last_z)

    def share(h, group, d):
        return ag(h, 20 + 4 * group + d, pieces[group](h, e, d), twin)

    def share_t(d):
        return ag(0, 36 + d, gt.at[e, :, (y + d) % 4], twin)

    pl.semaphore_wait(barrier, len(friends))
    for h in range(2):
        for copy in pre_x(h) + pre_z(h) + pre_y(h):
            copy.start()

    total = jnp.zeros((16, 512), F32)
    for k in range(32):
        part = refs[:, k * 512 : (k + 1) * 512].astype(F32)
        total = total + part * part
    ctf4 = jnp.concatenate([ctf[...]] * 4, axis=0)
    by_group = plain(0.5 * noise[...] * ctf4 * ctf4, spread, HIGHEST)
    energy = across(total, by_group, HIGHEST)
    high = energy.astype(BF16).astype(F32)
    middle = (energy - high).astype(BF16).astype(F32)
    low = energy - high - middle
    lane = lax.broadcasted_iota(jnp.int32, (16, 128), 1) // 32
    gt[e, zh, y] = jnp.where(
        lane == 0, high, jnp.where(lane == 1, middle, jnp.where(lane == 2, low, 0.0))
    ).astype(BF16)
    pre_t.start()

    index = (offsets[0:1, :] + 6) * SHIFTS + offsets[1:2, :] + 6
    index = jnp.transpose(jnp.broadcast_to(index.astype(F32), (128, IMG)))
    upper = SHIFTS * SHIFTS - 1.0
    sign[...] = jnp.where(index < KINDS, 1.0, -1.0)
    kind = jnp.minimum(index, upper - index)[:, 0:1]
    column = lax.broadcasted_iota(jnp.int32, (IMG, DEPTH), 1).astype(F32)
    hot[...] = ((column == kind) | (column == kind + LOW)).astype(F32).astype(BF16)
    of_group = (
        lax.broadcasted_iota(jnp.int32, (32, IMG), 0) == groups[...]
    ).astype(F32)
    cgt[...] = lax.dot_general(
        ctf[...], of_group, (((0,), (0,)), ((), ())), precision=HIGHEST, preferred_element_type=F32
    )

    def prepare(c):
        slot = c % 2
        if c < 3:
            spec_copy(c + 1).start()
            tab_copy(c + 1).start()
        spec_copy(c).wait()
        tab_copy(c).wait()

        @pl.loop(0, 16)
        def widen(b):
            part = spec[slot, pl.ds(b * 16, 16)].astype(F32)
            rows = pl.ds(pl.multiple_of(b * 256, 256), 256)
            qb[rows, :] = part[:, :, :A].reshape(256, A)
            rows = pl.ds(pl.multiple_of(4096 + b * 256, 256), 256)
            qb[rows, :] = part[:, :, A:].reshape(256, A)

        @pl.loop(0, 2)
        def move(b):
            for k in range(8):
                r = b * 8 + k
                turn = plain(hot[...], tab[slot, r])
                cosine, sine = turn[:, :A], turn[:, A:] * sign[...]
                real = qb[pl.ds(r, IMG, stride=16), :]
                imag = qb[pl.ds(4096 + r, IMG, stride=16), :]
                moved[r] = jnp.concatenate(
                    [real * cosine - imag * sine, real * sine + imag * cosine], axis=1
                ).astype(BF16)

        @pl.loop(0, 2)
        def transform(b):
            found = []
            for k in range(8):
                r = b * 8 + k
                out = across(harmonics[...], moved[r]) * cgt[pl.ds(c * 16 + r, 1), :]
                found.append(out.reshape(32, 8, IMG))
            both = jnp.concatenate(found, axis=1)
            ht[:, pl.ds(pl.multiple_of(c * 128 + b * 64, 64), 64), :] = both.astype(BF16)

    def pass_on(h):
        for copy in pre_x(h):
            copy.wait_recv()
        for d in (1, 3, 2):
            last_x(h, d).start()
        for copy in pre_z(h) + pre_y(h):
            copy.wait_recv()
        for d in (1, 3, 2):
            last_z(h, d).start()
            last_y(h, d).start()
        if h == 0:
            pre_t.wait_recv()
            for d in (1, 3, 2):
                last_t(d).start()
            share_t(0).start()
        for group in range(3):
            share(h, group, 0).start()

    def hand_over(h):
        for d in (1, 3, 2):
            for group in (1, 0, 2):
                lasts[group](h, d).wait_recv()
                share(h, group, d if group == 2 else 4 - d).start()
            if h == 0:
                last_t(d).wait_recv()
                share_t(4 - d).start()
        for d in range(4):
            for group in range(3):
                share(h, group, d).wait_recv()
            if h == 0:
                share_t(d).wait_recv()

    def correlate(h):
        @pl.loop(0, 4)
        def _(k):
            for zv in range(2):
                j = zv * 8 + k * 2 + h
                part_x = gx[:, :, :, k, h, zv].reshape(256, WX)
                part_y = gy[:, :, :, h, k, zv].reshape(256, WY)
                part_z = gz[:, :, :, zv, h, k].reshape(256, WZ)
                real = jnp.concatenate([part_x, part_y[:, :128]], axis=1)
                imag = jnp.concatenate([part_y[:, 128:], part_z], axis=1)
                h_re, h_im = ht[2 * j], ht[2 * j + 1]
                q_re = plain(real, h_re) + plain(imag, h_im)
                q_im = plain(imag, h_re) - plain(real, h_im)
                for t in range(2):
                    base = pl.multiple_of((t * 32 + 2 * j) * 256, 256)
                    qb[pl.ds(base, 256), :] = q_re[:, t * 128 : (t + 1) * 128]
                    qb[pl.ds(base + 256, 256), :] = q_im[:, t * 128 : (t + 1) * 128]

    prepare(0)
    pass_on(0)
    prepare(1)
    pass_on(1)
    prepare(2)
    prepare(3)
    hand_over(0)
    correlate(0)
    hand_over(1)
    correlate(1)

    row = lax.broadcasted_iota(jnp.int32, (128, IMG), 0)
    thrice = ((row % 32 == groups[...]) & (row < 96)).astype(F32).astype(BF16)
    norms = plain(gt[...].reshape(256, 128), thrice)
    norm[0:256, :] = norms[:, :128]
    norm[256:512, :] = norms[:, 128:]

    for t in range(2):
        def at(k, c, t=t):
            return (t * 32 + k) * 256 + c

        def scores(b, top, t=t, at=at):
            c = pl.multiple_of(b * 8, 8)
            re = [qb[pl.ds(at(2 * j, c), 8), :] for j in range(16)]
            im = [qb[pl.ds(at(2 * j + 1, c), 8), :] for j in range(16)]
            a = [re[0]] + [re[j] + re[16 - j] for j in range(1, 8)] + [re[8]]
            s = [None] + [im[j] - im[16 - j] for j in range(1, 8)]
            a[0] = a[0] - norm[pl.ds(t * 256 + c, 8), :]
            cp, sp = cosine_part(a), sine_part(s)
            out = [cp[0]] + [cp[k] + sp[k] for k in range(1, 8)] + [cp[8]]
            out += [cp[16 - k] - sp[16 - k] for k in range(9, 16)]
            for k in range(16):
                qb[pl.ds(at(k, c), 8), :] = out[k]
                top = jnp.maximum(top, out[k])
            return top

        top = lax.fori_loop(0, 32, scores, jnp.full((8, 128), -jnp.inf, F32))
        top = jnp.max(top, axis=0, keepdims=True)

        def exponents(b, total, top=top, at=at):
            c = pl.multiple_of(b * 8, 8)
            for k in range(16):
                value = jnp.exp(qb[pl.ds(at(k, c), 8), :] - top)
                qb[pl.ds(at(k, c), 8), :] = value
                total = total + value
            return total

        total = lax.fori_loop(0, 32, exponents, jnp.zeros((8, 128), F32))
        scale = 1.0 / jnp.sum(total, axis=0, keepdims=True)
        prob_out[:, t * 128 : (t + 1) * 128] = scale

        @pl.loop(0, 16)
        def back(b, t=t, at=at, scale=scale):
            c = pl.multiple_of(b * 16, 16)
            p = [qb[pl.ds(at(k, c), 16), :] * scale for k in range(16)]
            a = [p[0]] + [p[k] + p[16 - k] for k in range(1, 8)] + [p[8]]
            s = [None] + [p[k] - p[16 - k] for k in range(1, 8)]
            cp, sp = cosine_part(a), sine_part(s)
            cols = slice(t * 128, (t + 1) * 128)
            zero = jnp.zeros((16, 128), BF16)
            for j in range(9):
                re = cp[j].astype(BF16)
                wb[j, 0, pl.ds(c, 16), cols] = re
                if j in (0, 8):
                    wb[j, 1, pl.ds(c, 16), cols] = zero
                else:
                    wb[16 - j, 0, pl.ds(c, 16), cols] = re
                    wb[j, 1, pl.ds(c, 16), cols] = sp[j].astype(BF16)
                    wb[16 - j, 1, pl.ds(c, 16), cols] = (-sp[j]).astype(BF16)

    for h in range(2):
        for copy in pre_x(h) + pre_y(h) + pre_z(h):
            copy.wait_send()
        for group in range(3):
            for d in (1, 2, 3):
                lasts[group](h, d).wait_send()
            for d in range(4):
                share(h, group, d).wait_send()
    pre_t.wait_send()
    for d in (1, 2, 3):
        last_t(d).wait_send()
    for d in range(4):
        share_t(d).wait_send()

    def target(it):
        return (x + 1 + it) % 4, it // 4

    def trade(it):
        xt, h = target(it)
        pairs = (
            (gx.at[other, :, :, xt, h], cx.at[:, :, xt, h]),
            (gy.at[other, :, :, h, xt], cy.at[:, :, h, xt]),
            (gz.at[other, :, :, :, h, xt], cz.at[:, :, :, h, xt]),
        )
        return [
            remote(src, dst, core_s.at[k, it], core_r.at[k, it], twin)
            for k, (src, dst) in enumerate(pairs)
        ]

    def first_x(it):
        xt, h = target(it)
        u = it % 4
        return remote(
            gx.at[e, :, :, xt, h], rx1.at[u, h], x1_s.at[u, h], x1_r.at[u, h], at_x(u + 1)
        )

    def first_y(it, d):
        xt, h = target(it)
        return remote(
            gy.at[e, :, (y + d) % 4, h, xt], ry1.at[d - 1, h, :, xt],
            y1_s.at[d - 1, it], y1_r.at[d - 1, it], at_y(d),
        )

    def first_z(it, d):
        xt, h = target(it)
        zh_, zl_ = flip(d)
        return remote(
            gz.at[e, zh_, :, zl_, h, xt], rz1.at[d - 1, h, :, xt],
            z1_s.at[d - 1, it], z1_r.at[d - 1, it], at_z(d),
        )

    def settle(it):
        xt, h = target(it)
        for copy in trade(it):
            copy.wait_recv()

        @pl.loop(0, 8)
        def add(s):
            w, v = s // 4, s % 4
            gx[e, w, v, xt, h] = (
                gx[e, w, v, xt, h].astype(F32) + cx[w, v, xt, h].astype(F32)
            ).astype(BF16)
            gy[e, w, v, h, xt] = (
                gy[e, w, v, h, xt].astype(F32) + cy[w, v, h, xt].astype(F32)
            ).astype(BF16)
            gz[e, w, v, :, h, xt] = (
                gz[e, w, v, :, h, xt].astype(F32) + cz[w, v, :, h, xt].astype(F32)
            ).astype(BF16)

        @pl.when(it % 4 != 3)
        def _():
            first_x(it).start()

        for d in (1, 3, 2):
            first_z(it, d).start()
            first_y(it, d).start()

    @pl.loop(0, 8)
    def accumulate(it):
        xt, h = target(it)
        for zv in range(2):
            j = zv * 8 + xt * 2 + h
            w_re, w_im = wb[j, 0], wb[j, 1]
            w_minus = wb[(16 - j) % 16, 1]
            h_both = jnp.concatenate([ht[2 * j], ht[2 * j + 1]], axis=1)
            out_re = across(jnp.concatenate([w_re, w_minus], axis=1), h_both).astype(BF16)
            out_im = across(jnp.concatenate([w_im, w_re], axis=1), h_both).astype(BF16)
            gx[:, :, :, xt, h, zv] = out_re[:, :384].reshape(2, 2, 4, 16, WX)
            gy[:, :, :, h, xt, zv] = jnp.concatenate(
                [out_re[:, 384:], out_im[:, :128]], axis=1
            ).reshape(2, 2, 4, 16, WY)
            gz[:, :, :, zv, h, xt] = out_im[:, 128:].reshape(2, 2, 4, 16, WZ)
        for copy in trade(it):
            copy.start()

        @pl.when(it > 0)
        def _():
            settle(it - 1)

    settle(7)

    def late(stage, group, h, d, src, dst, where):
        return remote(
            src, dst.at[d - 1, h], late_s.at[stage, group, h, d - 1],
            late_r.at[stage, group, h, d - 1], where,
        )

    def second_x(h, d):
        return late(0, 0, h, d, gx.at[e, :, (y + d) % 4, x, h], rx2, at_y(d))

    def second_y(h, d):
        zh_, zl_ = flip(d)
        return late(0, 1, h, d, gy.at[e, zh_, y, h, :, zl_], ry2, at_z(d))

    def second_z(h, d):
        return late(0, 2, h, d, gz.at[e, zh, :, zl, h, (x + d) % 4], rz2, at_x(d))

    def third_x(h, d):
        zh_, zl_ = flip(d)
        return late(1, 0, h, d, gx.at[e, zh_, y, x, h, zl_], rx3, at_z(d))

    def third_y(h, d):
        return late(1, 1, h, d, gy.at[e, zh, y, h, (x + d) % 4, zl], ry3, at_x(d))

    def third_z(h, d):
        return late(1, 2, h, d, gz.at[e, zh, (y + d) % 4, zl, h, x], rz3, at_y(d))

    def total_of(own, parts):
        acc = own.astype(F32)
        for part in parts:
            acc = acc + part.astype(F32)
        return acc

    for h in range(2):
        for u in range(3):
            first_x(u + 4 * h).wait_recv()

        @pl.loop(0, 8)
        def add_x1(s, h=h):
            w, v = s // 4, s % 4
            gx[e, w, v, x, h] = total_of(
                gx[e, w, v, x, h], [rx1[u, h, w, v] for u in range(3)]
            ).astype(BF16)

        for d in (1, 3, 2):
            second_x(h, d).start()
        for it in range(4 * h, 4 * h + 4):
            for d in (1, 2, 3):
                first_z(it, d).wait_recv()

        @pl.loop(0, 4)
        def add_z1(v, h=h):
            gz[e, zh, v, zl, h] = total_of(
                gz[e, zh, v, zl, h], [rz1[d, h, v] for d in range(3)]
            ).astype(BF16)

        for d in (1, 3, 2):
            second_z(h, d).start()
        for it in range(4 * h, 4 * h + 4):
            for d in (1, 2, 3):
                first_y(it, d).wait_recv()

        @pl.loop(0, 8)
        def add_y1(s, h=h):
            w, k = s // 4, s % 4
            gy[e, w, y, h, k] = total_of(
                gy[e, w, y, h, k], [ry1[d, h, w, k] for d in range(3)]
            ).astype(BF16)

        for d in (1, 3, 2):
            second_y(h, d).start()

    for h in range(2):
        for d in (1, 3, 2):
            second_x(h, d).wait_recv()
        gx[e, :, y, x, h] = total_of(
            gx[e, :, y, x, h], [rx2[d, h] for d in range(3)]
        ).astype(BF16)
        for d in (1, 3, 2):
            third_x(h, d).start()
        for d in (1, 3, 2):
            second_z(h, d).wait_recv()
        gz[e, zh, :, zl, h, x] = total_of(
            gz[e, zh, :, zl, h, x], [rz2[d, h] for d in range(3)]
        ).astype(BF16)
        for d in (1, 3, 2):
            third_z(h, d).start()
        for d in (1, 3, 2):
            second_y(h, d).wait_recv()
        gy[e, zh, y, h, :, zl] = total_of(
            gy[e, zh, y, h, :, zl], [ry2[d, h] for d in range(3)]
        ).astype(BF16)
        for d in (1, 3, 2):
            third_y(h, d).start()

    for h in range(2):
        first = h * 1024
        for third in (third_x, third_z, third_y):
            for d in (1, 2, 3):
                third(h, d).wait_recv()
        sums_out[:, first : first + WX] = total_of(
            gx[e, zh, y, x, h, zl], [rx3[d, h] for d in range(3)]
        )
        sums_out[:, first + WX : first + WX + WY] = total_of(
            gy[e, zh, y, h, x, zl], [ry3[d, h] for d in range(3)]
        )
        sums_out[:, first + WX + WY : first + 1024] = total_of(
            gz[e, zh, y, zl, h, x], [rz3[d, h] for d in range(3)]
        )

    for it in range(8):
        for copy in trade(it):
            copy.wait_send()
        if it % 4 != 3:
            first_x(it).wait_send()
        for d in (1, 2, 3):
            first_y(it, d).wait_send()
            first_z(it, d).wait_send()
    for copy in (second_x, second_y, second_z, third_x, third_y, third_z):
        for h in range(2):
            for d in (1, 2, 3):
                copy(h, d).wait_send()


def on_device(spectra, offsets, groups, ctf, noise_weight, references):
    vmem = pl.BlockSpec(memory_space=pltpu.VMEM)
    anywhere = pl.BlockSpec(memory_space=pl.ANY)
    sem = pltpu.SemaphoreType.DMA
    sums, prob = pl.pallas_call(
        kernel,
        out_shape=(
            jax.ShapeDtypeStruct((16, 2048), F32),
            jax.ShapeDtypeStruct((1, IMG), F32),
        ),
        in_specs=[anywhere, anywhere] + [vmem] * 6,
        out_specs=(vmem, vmem),
        scratch_shapes=[
            pltpu.VMEM((2, 2, 4, 4, 2, 2, 16, WX), BF16),
            pltpu.VMEM((2, 2, 4, 2, 4, 2, 16, WY), BF16),
            pltpu.VMEM((2, 2, 4, 2, 2, 4, 16, WZ), BF16),
            pltpu.VMEM((2, 2, 4, 16, 128), BF16),
            pltpu.VMEM((2, 4, 4, 2, 2, 16, WX), BF16),
            pltpu.VMEM((2, 4, 2, 4, 2, 16, WY), BF16),
            pltpu.VMEM((2, 4, 2, 2, 4, 16, WZ), BF16),
            pltpu.VMEM((32, 512, IMG), BF16),
            pltpu.VMEM((16384, 128), F32),
            pltpu.VMEM((16, 2, 256, IMG), BF16),
            pltpu.VMEM((512, 128), F32),
            pltpu.VMEM((2, IMG, 16, 2 * A), BF16),
            pltpu.VMEM((2, 16, DEPTH, 2 * A), BF16),
            pltpu.VMEM((16, IMG, 2 * A), BF16),
            pltpu.VMEM((IMG, DEPTH), BF16),
            pltpu.VMEM((IMG, A), F32),
            pltpu.VMEM((R, IMG), F32),
            pltpu.VMEM((3, 2, 2, 4, 2, 16, WX), BF16),
            pltpu.VMEM((3, 2, 2, 4, 2, 16, WY), BF16),
            pltpu.VMEM((3, 2, 4, 4, 16, WZ), BF16),
            pltpu.VMEM((3, 2, 2, 2, 16, WX), BF16),
            pltpu.VMEM((3, 2, 4, 16, WY), BF16),
            pltpu.VMEM((3, 2, 4, 16, WZ), BF16),
            pltpu.VMEM((3, 2, 16, WX), BF16),
            pltpu.VMEM((3, 2, 16, WY), BF16),
            pltpu.VMEM((3, 2, 16, WZ), BF16),
            sem((4,)),
            sem((2, 40)),
            sem((2, 40)),
            sem((3, 8)),
            sem((3, 8)),
            sem((3, 2)),
            sem((3, 2)),
            sem((3, 8)),
            sem((3, 8)),
            sem((3, 8)),
            sem((3, 8)),
            sem((2, 3, 2, 3)),
            sem((2, 3, 2, 3)),
        ],
        compiler_params=pltpu.CompilerParams(
            collective_id=0, has_side_effects=True, vmem_limit_bytes=60 << 20
        ),
        cost_estimate=pl.CostEstimate(
            flops=14 << 30, bytes_accessed=24 << 20, transcendentals=1 << 20
        ),
        name="classify",
    )(
        spectra,
        jnp.asarray(shift_table()),
        offsets.T,
        groups.reshape(1, -1),
        ctf,
        noise_weight.reshape(1, -1),
        references,
        jnp.asarray(harmonic_rows()),
    )
    return sums, prob.reshape(-1)


def solution(mesh):
    placed = (
        P(("img", "cls"), None, None),
        P(("img", "cls"), None),
        P(("img", "cls")),
        P(),
        P(),
        P("cls", None),
    )
    return jax.shard_map(
        on_device,
        mesh=mesh,
        in_specs=placed,
        out_specs=(P("cls", "img"), P(("img", "cls"))),
        check_vma=False,
    )
```

```python
import math

import jax
import jax.numpy as jnp
import ml_dtypes
import numpy as np
from jax import lax
from jax.experimental import pallas as pl
from jax.experimental.pallas import tpu as pltpu
from jax.sharding import PartitionSpec as P

MESH = pl.DeviceIdType.MESH
F32 = jnp.float32
BF16 = jnp.bfloat16
HIGHEST = lax.Precision.HIGHEST

IMG = 256
R = 64
A = 128
ROTS = 16
SHIFTS = 13
KINDS = (SHIFTS * SHIFTS + 1) // 2
LOW = 88
DEPTH = 176
WX, WY, WZ = 384, 256, 384

SETTLE, FINISH = 3, 6

S1 = math.sqrt(0.5)
C1 = math.cos(math.pi / 8)
C3 = math.cos(3 * math.pi / 8)


def split_np(values):
    high = values.astype(np.float32).astype(ml_dtypes.bfloat16)
    low = (values - high.astype(np.float64)).astype(np.float32).astype(ml_dtypes.bfloat16)
    return high, low


def shift_table():
    theta = 2.0 * np.pi * np.arange(A) / A
    radius = np.arange(R) + 1.0
    step = np.arange(SHIFTS) - 6.0
    along = (
        np.cos(theta)[None, None, :] * step[:, None, None]
        + np.sin(theta)[None, None, :] * step[None, :, None]
    ).reshape(SHIFTS * SHIFTS, A)[:KINDS]
    phase = -2.0 * np.pi * radius[:, None, None] * along[None] / (2.0 * R)
    both = np.concatenate([np.cos(phase), np.sin(phase)], axis=-1)
    high, low = split_np(both)
    table = np.zeros((R, DEPTH, 2 * A), ml_dtypes.bfloat16)
    table[:, :KINDS] = high
    table[:, LOW : LOW + KINDS] = low
    return table


def harmonic_rows():
    quarter = A // ROTS
    orders = ROTS * np.arange(quarter)[None, :] + np.arange(ROTS)[:, None]
    turns = (np.arange(A)[:, None, None] * orders[None]) % A
    angle = 2.0 * np.pi * turns / A
    upper = np.stack([np.cos(angle), -np.sin(angle)], axis=2)
    lower = np.stack([np.sin(angle), np.cos(angle)], axis=2)
    table = np.concatenate([upper, lower], axis=0) / math.sqrt(A)
    return np.ascontiguousarray(table.reshape(2 * A, 2 * A).T).astype(np.float32).astype(
        ml_dtypes.bfloat16
    )


def cosine_part(a):
    p, m = a[0] + a[8], a[0] - a[8]
    t, d = a[2] + a[6], S1 * (a[2] - a[6])
    q = p + a[4]
    even = [q + t, m + d, p - a[4], m - d, q - t]
    s17, d17 = a[1] + a[7], a[1] - a[7]
    s35, d35 = a[3] + a[5], a[3] - a[5]
    odd = [s17 + s35, C1 * d17 + C3 * d35, S1 * (s17 - s35), C3 * d17 - C1 * d35]
    out = [even[k] + odd[k] for k in range(4)] + [even[4]]
    return out + [even[k] - odd[k] for k in (3, 2, 1, 0)]


def sine_part(b):
    t = S1 * (b[2] + b[6])
    even = [None, t + b[4], b[2] - b[6], t - b[4]]
    s17, d17 = b[1] + b[7], b[1] - b[7]
    s35, d35 = b[3] + b[5], b[3] - b[5]
    odd = [None, C3 * s17 + C1 * s35, S1 * (d17 + d35), C1 * s17 - C3 * s35, d17 - d35]
    out = [None] + [odd[k] + even[k] for k in (1, 2, 3)] + [odd[4]]
    return out + [odd[k] - even[k] for k in (3, 2, 1)]


def across(a, b, precision=None):
    return lax.dot_general(
        a, b, (((1,), (1,)), ((), ())), precision=precision, preferred_element_type=F32
    )


def plain(a, b, precision=None):
    return jnp.dot(a, b, precision=precision, preferred_element_type=F32)


def kernel(
    spectra, table, offsets, groups, ctf, noise, refs, harmonics,
    sums_out, prob_out,
    gx, gy, gz, gt, cx, cy, cz, ht, qb, wb, norm, spec, tab, moved, hot, sign, cgt,
    qx, qz, rx1, ry1, rz1, rx2, ry2, rz2, rx3, ry3, rz3,
    dma, ag_s, ag_r, core_s, core_r, qx_s, qx_r, qz_s, qz_r,
    x1_s, x1_r, y1_s, y1_r, z1_s, z1_r, late_s, late_r,
):
    img = lax.axis_index("img")
    cls = lax.axis_index("cls")
    zl, x = img // 4, img % 4
    zh, y, e = cls // 8, (cls // 2) % 4, cls % 2
    other = 1 - e

    def device(zl_, x_, zh_, y_, e_):
        return (zl_ * 4 + x_, zh_ * 8 + y_ * 2 + e_)

    def at_x(d):
        return device(zl, (x + d) % 4, zh, y, e)

    def at_y(d):
        return device(zl, x, zh, (y + d) % 4, e)

    def flip(d):
        return (zh + d // 2) % 2, (zl + d) % 2

    def at_z(d):
        zh_, zl_ = flip(d)
        return device(zl_, x, zh_, y, e)

    twin = device(zl, x, zh, y, other)

    def remote(src, dst, send, recv, where):
        return pltpu.make_async_remote_copy(
            src_ref=src, dst_ref=dst, send_sem=send, recv_sem=recv,
            device_id=where, device_id_type=MESH,
        )

    def spec_copy(c):
        return pltpu.make_async_copy(
            spectra.at[:, pl.ds(c * 16, 16), :], spec.at[c % 2], dma.at[c % 2]
        )

    def tab_copy(c):
        return pltpu.make_async_copy(
            table.at[pl.ds(c * 16, 16)], tab.at[c % 2], dma.at[2 + c % 2]
        )

    barrier = pltpu.get_barrier_semaphore()
    friends = [twin]
    friends += [at_x(d) for d in (1, 2, 3)]
    friends += [at_y(d) for d in (1, 2, 3)]
    friends += [at_z(d) for d in (1, 2, 3)]
    for friend in friends:
        pl.semaphore_signal(barrier, inc=1, device_id=friend, device_id_type=MESH)
    spec_copy(0).start()
    tab_copy(0).start()

    spread = (
        lax.broadcasted_iota(jnp.int32, (R, 512), 0)
        == lax.broadcasted_iota(jnp.int32, (R, 512), 1) // 8
    ).astype(F32)
    nw = jnp.broadcast_to(noise[...], (8, R))
    nwx = plain(nw, spread, HIGHEST)[0:1]

    def weighted(j, first, width, gains):
        start = j * 1024 + first
        part = refs[:, pl.ds(pl.multiple_of(start, 128), width)].astype(F32)
        return (part * gains).astype(BF16)

    gain_x = nwx[:, :384]
    gain_y = jnp.concatenate([nwx[:, 384:], nwx[:, :128]], axis=1)
    gain_z = nwx[:, 128:]
    for h in range(2):
        for k in range(2):
            gx[e, zh, y, x, h, k] = weighted(k * 8 + x * 2 + h, 0, WX, gain_x)
        for k in range(4):
            gz[e, zh, y, zl, h, k] = weighted(zl * 8 + k * 2 + h, WX + WY, WZ, gain_z)
        for k in range(8):
            gy[e, zh, y, h, k // 2, k % 2] = weighted(
                (k % 2) * 8 + (k // 2) * 2 + h, WX, WY, gain_y
            )

    def ag(h, index, piece, where):
        return remote(piece, piece, ag_s.at[h, index], ag_r.at[h, index], where)

    def flip_x(h):
        return ag(h, 3, gx.at[e, zh, y, x, h], at_z(3))

    def pre_x(h):
        return [ag(h, d - 1, gx.at[e, :, y, x, h], at_y(d)) for d in (1, 3, 2)]

    def pre_z(h):
        return [ag(h, 6 + d, gz.at[e, zh, y, zl, h], at_y(d)) for d in (1, 3, 2)]

    def pre_y(h):
        return [ag(h, 10, gy.at[e, zh, y, h], at_z(3))]

    pre_t = ag(0, 32, gt.at[e, zh, y], at_z(3))

    def piece_x(h, e_, d):
        return gx.at[e_, :, :, (x + d) % 4, h]

    def piece_y(h, e_, d):
        return gy.at[e_, :, (y + d) % 4, h]

    def piece_z(h, e_, d):
        zh_, zl_ = flip(d)
        return gz.at[e_, zh_, :, zl_, h]

    def last_x(h, d):
        return ag(h, 10 + d, piece_x(h, e, 0), at_x(d))

    def last_y(h, d):
        return ag(h, 13 + d, piece_y(h, e, 0), at_y(d))

    def last_z(h, d):
        return ag(h, 16 + d, piece_z(h, e, 0), at_z(d))

    def relays(h):
        z_1, z_3 = flip(1), flip(3)
        return [
            ag(h, 4, gx.at[e, 0, :, (x + 3) % 4, h], at_x(1)),
            ag(h, 5, gx.at[e, 1, :, (x + 1) % 4, h], at_x(3)),
            ag(h, 6, gy.at[e, 0, (y + 3) % 4, h], at_y(1)),
            ag(h, 12, gy.at[e, 1, (y + 1) % 4, h], at_y(3)),
            ag(h, 15, gz.at[e, z_3[0], pl.ds(0, 2), z_3[1], h], at_z(1)),
            ag(h, 18, gz.at[e, z_1[0], pl.ds(2, 2), z_1[1], h], at_z(3)),
        ]

    def last_t(d):
        return ag(0, 32 + d, gt.at[e, :, y], at_y(d))

    pieces = (piece_x, piece_y, piece_z)
    lasts = (last_x, last_y, last_z)

    def share(h, group, d):
        return ag(h, 20 + 4 * group + d, pieces[group](h, e, d), twin)

    def share_t(d):
        return ag(0, 36 + d, gt.at[e, :, (y + d) % 4], twin)

    pl.semaphore_wait(barrier, len(friends))
    flip_x(0).start()
    flip_x(1).start()
    for h in range(2):
        for copy in pre_z(h) + pre_y(h):
            copy.start()
        flip_x(h).wait_recv()
        for copy in pre_x(h):
            copy.start()

    total = jnp.zeros((16, 512), F32)
    for k in range(32):
        part = refs[:, k * 512 : (k + 1) * 512].astype(F32)
        total = total + part * part
    ctf4 = jnp.concatenate([ctf[...]] * 4, axis=0)
    by_group = plain(0.5 * noise[...] * ctf4 * ctf4, spread, HIGHEST)
    energy = across(total, by_group, HIGHEST)
    high = energy.astype(BF16).astype(F32)
    middle = (energy - high).astype(BF16).astype(F32)
    low = energy - high - middle
    lane = lax.broadcasted_iota(jnp.int32, (16, 128), 1) // 32
    gt[e, zh, y] = jnp.where(
        lane == 0, high, jnp.where(lane == 1, middle, jnp.where(lane == 2, low, 0.0))
    ).astype(BF16)
    pre_t.start()

    index = (offsets[0:1, :] + 6) * SHIFTS + offsets[1:2, :] + 6
    index = jnp.transpose(jnp.broadcast_to(index.astype(F32), (128, IMG)))
    upper = SHIFTS * SHIFTS - 1.0
    sign[...] = jnp.where(index < KINDS, 1.0, -1.0)
    kind = jnp.minimum(index, upper - index)[:, 0:1]
    column = lax.broadcasted_iota(jnp.int32, (IMG, DEPTH), 1).astype(F32)
    hot[...] = ((column == kind) | (column == kind + LOW)).astype(F32).astype(BF16)
    of_group = (
        lax.broadcasted_iota(jnp.int32, (32, IMG), 0) == groups[...]
    ).astype(F32)
    cgt[...] = lax.dot_general(
        ctf[...], of_group, (((0,), (0,)), ((), ())), precision=HIGHEST, preferred_element_type=F32
    )

    def prepare(c):
        slot = c % 2
        if c < 3:
            spec_copy(c + 1).start()
            tab_copy(c + 1).start()
        spec_copy(c).wait()
        tab_copy(c).wait()

        @pl.loop(0, 16)
        def widen(b):
            part = spec[slot, pl.ds(b * 16, 16)].astype(F32)
            rows = pl.ds(pl.multiple_of(b * 256, 256), 256)
            qb[rows, :] = part[:, :, :A].reshape(256, A)
            rows = pl.ds(pl.multiple_of(4096 + b * 256, 256), 256)
            qb[rows, :] = part[:, :, A:].reshape(256, A)

        @pl.loop(0, 2)
        def move(b):
            for k in range(8):
                r = b * 8 + k
                turn = plain(hot[...], tab[slot, r])
                cosine, sine = turn[:, :A], turn[:, A:] * sign[...]
                real = qb[pl.ds(r, IMG, stride=16), :]
                imag = qb[pl.ds(4096 + r, IMG, stride=16), :]
                moved[r] = jnp.concatenate(
                    [real * cosine - imag * sine, real * sine + imag * cosine], axis=1
                ).astype(BF16)

        @pl.loop(0, 2)
        def transform(b):
            found = []
            for k in range(8):
                r = b * 8 + k
                out = across(harmonics[...], moved[r]) * cgt[pl.ds(c * 16 + r, 1), :]
                found.append(out.reshape(32, 8, IMG))
            both = jnp.concatenate(found, axis=1)
            ht[:, pl.ds(pl.multiple_of(c * 128 + b * 64, 64), 64), :] = both.astype(BF16)

    def pass_on(h):
        for copy in pre_x(h):
            copy.wait_recv()
        for d in (1, 3):
            last_x(h, d).start()
        for copy in pre_z(h) + pre_y(h):
            copy.wait_recv()
        for d in (1, 3):
            last_z(h, d).start()
            last_y(h, d).start()
        if h == 0:
            pre_t.wait_recv()
            for d in (1, 3, 2):
                last_t(d).start()
            share_t(0).start()
        for group in range(3):
            share(h, group, 0).start()

    def relay(h):
        moves = relays(h)
        for k, (group, d) in enumerate(((0, 1), (0, 3), (1, 1), (1, 3), (2, 3), (2, 1))):
            lasts[group](h, d).wait_recv()
            moves[k].start()
            share(h, group, d if group == 2 else 4 - d).start()

    def hand_over(h):
        moves = relays(h)
        for group in range(3):
            moves[2 * group].wait_recv()
            moves[2 * group + 1].wait_recv()
            share(h, group, 2).start()
        if h == 0:
            for d in (1, 3, 2):
                last_t(d).wait_recv()
                share_t(4 - d).start()
        for d in (0, 1, 3, 2):
            for group in range(3):
                share(h, group, d).wait_recv()
            if h == 0:
                share_t(d).wait_recv()

    def correlate(h):
        @pl.loop(0, 4)
        def _(k):
            for zv in range(2):
                j = zv * 8 + k * 2 + h
                part_x = gx[:, :, :, k, h, zv].reshape(256, WX)
                part_y = gy[:, :, :, h, k, zv].reshape(256, WY)
                part_z = gz[:, :, :, zv, h, k].reshape(256, WZ)
                real = jnp.concatenate([part_x, part_y[:, :128]], axis=1)
                imag = jnp.concatenate([part_y[:, 128:], part_z], axis=1)
                h_re, h_im = ht[2 * j], ht[2 * j + 1]
                q_re = plain(real, h_re) + plain(imag, h_im)
                q_im = plain(imag, h_re) - plain(real, h_im)
                for t in range(2):
                    base = pl.multiple_of((t * 32 + 2 * j) * 256, 256)
                    qb[pl.ds(base, 256), :] = q_re[:, t * 128 : (t + 1) * 128]
                    qb[pl.ds(base + 256, 256), :] = q_im[:, t * 128 : (t + 1) * 128]

    prepare(0)
    pass_on(0)
    prepare(1)
    pass_on(1)
    prepare(2)
    relay(0)
    prepare(3)
    relay(1)
    hand_over(0)
    correlate(0)
    hand_over(1)
    correlate(1)

    row = lax.broadcasted_iota(jnp.int32, (128, IMG), 0)
    thrice = ((row % 32 == groups[...]) & (row < 96)).astype(F32).astype(BF16)
    norms = plain(gt[...].reshape(256, 128), thrice)
    norm[0:256, :] = norms[:, :128]
    norm[256:512, :] = norms[:, 128:]

    for t in range(2):
        def at(k, c, t=t):
            return (t * 32 + k) * 256 + c

        def scores(b, top, t=t, at=at):
            c = pl.multiple_of(b * 8, 8)
            re = [qb[pl.ds(at(2 * j, c), 8), :] for j in range(16)]
            im = [qb[pl.ds(at(2 * j + 1, c), 8), :] for j in range(16)]
            a = [re[0]] + [re[j] + re[16 - j] for j in range(1, 8)] + [re[8]]
            s = [None] + [im[j] - im[16 - j] for j in range(1, 8)]
            a[0] = a[0] - norm[pl.ds(t * 256 + c, 8), :]
            cp, sp = cosine_part(a), sine_part(s)
            out = [cp[0]] + [cp[k] + sp[k] for k in range(1, 8)] + [cp[8]]
            out += [cp[16 - k] - sp[16 - k] for k in range(9, 16)]
            for k in range(16):
                qb[pl.ds(at(k, c), 8), :] = out[k]
                top = jnp.maximum(top, out[k])
            return top

        top = lax.fori_loop(0, 32, scores, jnp.full((8, 128), -jnp.inf, F32))
        top = jnp.max(top, axis=0, keepdims=True)

        def exponents(b, total, top=top, at=at):
            c = pl.multiple_of(b * 8, 8)
            for k in range(16):
                value = jnp.exp(qb[pl.ds(at(k, c), 8), :] - top)
                qb[pl.ds(at(k, c), 8), :] = value
                total = total + value
            return total

        total = lax.fori_loop(0, 32, exponents, jnp.zeros((8, 128), F32))
        scale = 1.0 / jnp.sum(total, axis=0, keepdims=True)
        prob_out[:, t * 128 : (t + 1) * 128] = scale

        @pl.loop(0, 16)
        def back(b, t=t, at=at, scale=scale):
            c = pl.multiple_of(b * 16, 16)
            p = [qb[pl.ds(at(k, c), 16), :] * scale for k in range(16)]
            a = [p[0]] + [p[k] + p[16 - k] for k in range(1, 8)] + [p[8]]
            s = [None] + [p[k] - p[16 - k] for k in range(1, 8)]
            cp, sp = cosine_part(a), sine_part(s)
            cols = slice(t * 128, (t + 1) * 128)
            zero = jnp.zeros((16, 128), BF16)
            for j in range(9):
                re = cp[j].astype(BF16)
                wb[j, 0, pl.ds(c, 16), cols] = re
                if j in (0, 8):
                    wb[j, 1, pl.ds(c, 16), cols] = zero
                else:
                    wb[16 - j, 0, pl.ds(c, 16), cols] = re
                    wb[j, 1, pl.ds(c, 16), cols] = sp[j].astype(BF16)
                    wb[16 - j, 1, pl.ds(c, 16), cols] = (-sp[j]).astype(BF16)

    for h in range(2):
        for copy in [flip_x(h)] + pre_x(h) + pre_y(h) + pre_z(h) + relays(h):
            copy.wait_send()
        for group in range(3):
            for d in (1, 3):
                lasts[group](h, d).wait_send()
            for d in range(4):
                share(h, group, d).wait_send()
    pre_t.wait_send()
    for d in (1, 2, 3):
        last_t(d).wait_send()
    for d in range(4):
        share_t(d).wait_send()

    def choose(it, values):
        out = values[0]
        for k in range(1, 8):
            out = jnp.where(it == k, values[k], out)
        return out

    def step_of(it):
        return choose(it, (2, 1, 3, 2, 0, 1, 3, 0)), choose(it, (0, 0, 0, 1, 0, 1, 1, 1))

    def target(it):
        step, h = step_of(it)
        return (x + step) % 4, h

    def trade(it):
        xt, h = target(it)
        pairs = (
            (gx.at[other, :, :, xt, h], cx.at[:, :, xt, h]),
            (gy.at[other, :, :, h, xt], cy.at[:, :, h, xt]),
            (gz.at[other, :, :, :, h, xt], cz.at[:, :, :, h, xt]),
        )
        return [
            remote(src, dst, core_s.at[k, it], core_r.at[k, it], twin)
            for k, (src, dst) in enumerate(pairs)
        ]

    def half_x(h, k):
        return remote(
            gx.at[e, k, :, (x + 2) % 4, h], qx.at[k, h], qx_s.at[k, h], qx_r.at[k, h],
            at_x(1 + 2 * k),
        )

    def half_z(it, k):
        xt, h = target(it)
        zh_, zl_ = flip(2)
        return remote(
            gz.at[e, zh_, pl.ds(2 * k, 2), zl_, h, xt], qz.at[k, it],
            qz_s.at[k, it], qz_r.at[k, it], at_z(1 + 2 * k),
        )

    def first_x(h, k):
        return remote(
            gx.at[e, :, :, (x + 1 + 2 * k) % 4, h], rx1.at[k, h],
            x1_s.at[k, h], x1_r.at[k, h], at_x(1 + 2 * k),
        )

    def first_y(it, d):
        xt, h = target(it)
        return remote(
            gy.at[e, :, (y + d) % 4, h, xt], ry1.at[d - 1, h, :, xt],
            y1_s.at[d - 1, it], y1_r.at[d - 1, it], at_y(d),
        )

    def first_z(it, k):
        xt, h = target(it)
        zh_, zl_ = flip(1 + 2 * k)
        return remote(
            gz.at[e, zh_, :, zl_, h, xt], rz1.at[k, h, :, xt],
            z1_s.at[k, it], z1_r.at[k, it], at_z(1 + 2 * k),
        )

    def settle(it):
        xt, h = target(it)
        for copy in trade(it):
            copy.wait_recv()

        @pl.loop(0, 8)
        def add(s):
            w, v = s // 4, s % 4
            gx[e, w, v, xt, h] = (
                gx[e, w, v, xt, h].astype(F32) + cx[w, v, xt, h].astype(F32)
            ).astype(BF16)
            gy[e, w, v, h, xt] = (
                gy[e, w, v, h, xt].astype(F32) + cy[w, v, h, xt].astype(F32)
            ).astype(BF16)
            gz[e, w, v, :, h, xt] = (
                gz[e, w, v, :, h, xt].astype(F32) + cz[w, v, :, h, xt].astype(F32)
            ).astype(BF16)

        @pl.when((it == 0) | (it == 3))
        def _():
            half_x(h, 0).start()
            half_x(h, 1).start()

        for k in range(2):
            half_z(it, k).start()
        for d in (1, 3, 2):
            first_y(it, d).start()

    def finish(it):
        xt, h = target(it)
        for k in range(2):
            @pl.when((it == 1 + k) | (it == 5 + k))
            def _(k=k):
                half_x(h, k).wait_recv()
                gx[e, k, :, xt, h] = (
                    gx[e, k, :, xt, h].astype(F32) + qx[k, h].astype(F32)
                ).astype(BF16)
                first_x(h, k).start()

        for k in range(2):
            half_z(it, k).wait_recv()
            zh_, zl_ = flip(3 - 2 * k)
            at = pl.ds(2 * k, 2)
            gz[e, zh_, at, zl_, h, xt] = (
                gz[e, zh_, at, zl_, h, xt].astype(F32) + qz[k, it].astype(F32)
            ).astype(BF16)
            first_z(it, 1 - k).start()

    def accumulate(it):
        xt, h = target(it)
        for zv in range(2):
            j = zv * 8 + xt * 2 + h
            w_re, w_im = wb[j, 0], wb[j, 1]
            w_minus = wb[(16 - j) % 16, 1]
            h_both = jnp.concatenate([ht[2 * j], ht[2 * j + 1]], axis=1)
            out_re = across(jnp.concatenate([w_re, w_minus], axis=1), h_both).astype(BF16)
            out_im = across(jnp.concatenate([w_im, w_re], axis=1), h_both).astype(BF16)
            gx[:, :, :, xt, h, zv] = out_re[:, :384].reshape(2, 2, 4, 16, WX)
            gy[:, :, :, h, xt, zv] = jnp.concatenate(
                [out_re[:, 384:], out_im[:, :128]], axis=1
            ).reshape(2, 2, 4, 16, WY)
            gz[:, :, :, zv, h, xt] = out_im[:, 128:].reshape(2, 2, 4, 16, WZ)
        for copy in trade(it):
            copy.start()

    @pl.loop(0, 8 + FINISH)
    def steps(it):
        @pl.when(it < 8)
        def _():
            accumulate(it)

        @pl.when((it >= SETTLE) & (it < 8 + SETTLE))
        def _():
            settle(it - SETTLE)

        @pl.when(it >= FINISH)
        def _():
            finish(it - FINISH)

    def late(stage, group, h, d, src, dst, where):
        return remote(
            src, dst.at[d - 1, h], late_s.at[stage, group, h, d - 1],
            late_r.at[stage, group, h, d - 1], where,
        )

    def second_x(h, d):
        return late(0, 0, h, d, gx.at[e, :, (y + d) % 4, x, h], rx2, at_y(d))

    def second_y(h, d):
        zh_, zl_ = flip(d)
        return late(0, 1, h, d, gy.at[e, zh_, y, h, :, zl_], ry2, at_z(d))

    def second_z(h, d):
        return late(0, 2, h, d, gz.at[e, zh, :, zl, h, (x + d) % 4], rz2, at_x(d))

    def third_x(h, d):
        zh_, zl_ = flip(d)
        return late(1, 0, h, d, gx.at[e, zh_, y, x, h, zl_], rx3, at_z(d))

    def third_y(h, d):
        return late(1, 1, h, d, gy.at[e, zh, y, h, (x + d) % 4, zl], ry3, at_x(d))

    def third_z(h, d):
        return late(1, 2, h, d, gz.at[e, zh, (y + d) % 4, zl, h, x], rz3, at_y(d))

    def total_of(own, parts):
        acc = own.astype(F32)
        for part in parts:
            acc = acc + part.astype(F32)
        return acc

    for h in range(2):
        for k in range(2):
            first_x(h, k).wait_recv()

        @pl.loop(0, 8)
        def add_x1(s, h=h):
            w, v = s // 4, s % 4
            gx[e, w, v, x, h] = total_of(
                gx[e, w, v, x, h], [rx1[k, h, w, v] for k in range(2)]
            ).astype(BF16)

        for d in (1, 3, 2):
            second_x(h, d).start()
        for it in ((0, 1, 2, 4), (3, 5, 6, 7))[h]:
            for k in range(2):
                first_z(it, k).wait_recv()

        @pl.loop(0, 4)
        def add_z1(v, h=h):
            gz[e, zh, v, zl, h] = total_of(
                gz[e, zh, v, zl, h], [rz1[k, h, v] for k in range(2)]
            ).astype(BF16)

        for d in (1, 3, 2):
            second_z(h, d).start()
        for it in ((0, 1, 2, 4), (3, 5, 6, 7))[h]:
            for d in (1, 2, 3):
                first_y(it, d).wait_recv()

        @pl.loop(0, 8)
        def add_y1(s, h=h):
            w, v = s // 4, s % 4
            gy[e, w, y, h, v] = total_of(
                gy[e, w, y, h, v], [ry1[d, h, w, v] for d in range(3)]
            ).astype(BF16)

        for d in (1, 3, 2):
            second_y(h, d).start()

    for h in range(2):
        for d in (1, 3, 2):
            second_x(h, d).wait_recv()
        gx[e, :, y, x, h] = total_of(
            gx[e, :, y, x, h], [rx2[d, h] for d in range(3)]
        ).astype(BF16)
        for d in (1, 3, 2):
            third_x(h, d).start()
        for d in (1, 3, 2):
            second_z(h, d).wait_recv()
        gz[e, zh, :, zl, h, x] = total_of(
            gz[e, zh, :, zl, h, x], [rz2[d, h] for d in range(3)]
        ).astype(BF16)
        for d in (1, 3, 2):
            third_z(h, d).start()
        for d in (1, 3, 2):
            second_y(h, d).wait_recv()
        gy[e, zh, y, h, :, zl] = total_of(
            gy[e, zh, y, h, :, zl], [ry2[d, h] for d in range(3)]
        ).astype(BF16)
        for d in (1, 3, 2):
            third_y(h, d).start()

    for h in range(2):
        first = h * 1024
        for third in (third_x, third_z, third_y):
            for d in (1, 2, 3):
                third(h, d).wait_recv()
        sums_out[:, first : first + WX] = total_of(
            gx[e, zh, y, x, h, zl], [rx3[d, h] for d in range(3)]
        )
        sums_out[:, first + WX : first + WX + WY] = total_of(
            gy[e, zh, y, h, x, zl], [ry3[d, h] for d in range(3)]
        )
        sums_out[:, first + WX + WY : first + 1024] = total_of(
            gz[e, zh, y, zl, h, x], [rz3[d, h] for d in range(3)]
        )

    for it in range(8):
        for copy in trade(it):
            copy.wait_send()
        for k in range(2):
            half_z(it, k).wait_send()
            first_z(it, k).wait_send()
        for d in (1, 2, 3):
            first_y(it, d).wait_send()
    for h in range(2):
        for k in range(2):
            half_x(h, k).wait_send()
            first_x(h, k).wait_send()
    for copy in (second_x, second_y, second_z, third_x, third_y, third_z):
        for h in range(2):
            for d in (1, 2, 3):
                copy(h, d).wait_send()


def write(sums, prob, sums_out, prob_out):
    sums_out[...] = sums[...]
    prob_out[...] = prob[...]


def on_device(spectra, offsets, groups, ctf, noise_weight, references):
    vmem = pl.BlockSpec(memory_space=pltpu.VMEM)
    anywhere = pl.BlockSpec(memory_space=pl.ANY)
    sem = pltpu.SemaphoreType.DMA
    sums, prob = pl.pallas_call(
        kernel,
        out_shape=(
            jax.ShapeDtypeStruct((16, 2048), F32),
            jax.ShapeDtypeStruct((1, IMG), F32),
        ),
        in_specs=[anywhere, anywhere] + [vmem] * 6,
        out_specs=(vmem, vmem),
        scratch_shapes=[
            pltpu.VMEM((2, 2, 4, 4, 2, 2, 16, WX), BF16),
            pltpu.VMEM((2, 2, 4, 2, 4, 2, 16, WY), BF16),
            pltpu.VMEM((2, 2, 4, 2, 2, 4, 16, WZ), BF16),
            pltpu.VMEM((2, 2, 4, 16, 128), BF16),
            pltpu.VMEM((2, 4, 4, 2, 2, 16, WX), BF16),
            pltpu.VMEM((2, 4, 2, 4, 2, 16, WY), BF16),
            pltpu.VMEM((2, 4, 2, 2, 4, 16, WZ), BF16),
            pltpu.VMEM((32, 512, IMG), BF16),
            pltpu.VMEM((16384, 128), F32),
            pltpu.VMEM((16, 2, 256, IMG), BF16),
            pltpu.VMEM((512, 128), F32),
            pltpu.VMEM((2, IMG, 16, 2 * A), BF16),
            pltpu.VMEM((2, 16, DEPTH, 2 * A), BF16),
            pltpu.VMEM((16, IMG, 2 * A), BF16),
            pltpu.VMEM((IMG, DEPTH), BF16),
            pltpu.VMEM((IMG, A), F32),
            pltpu.VMEM((R, IMG), F32),
            pltpu.VMEM((2, 2, 4, 2, 16, WX), BF16),
            pltpu.VMEM((2, 8, 2, 16, WZ), BF16),
            pltpu.VMEM((2, 2, 2, 4, 2, 16, WX), BF16),
            pltpu.VMEM((3, 2, 2, 4, 2, 16, WY), BF16),
            pltpu.VMEM((2, 2, 4, 4, 16, WZ), BF16),
            pltpu.VMEM((3, 2, 2, 2, 16, WX), BF16),
            pltpu.VMEM((3, 2, 4, 16, WY), BF16),
            pltpu.VMEM((3, 2, 4, 16, WZ), BF16),
            pltpu.VMEM((3, 2, 16, WX), BF16),
            pltpu.VMEM((3, 2, 16, WY), BF16),
            pltpu.VMEM((3, 2, 16, WZ), BF16),
            sem((4,)),
            sem((2, 40)),
            sem((2, 40)),
            sem((3, 8)),
            sem((3, 8)),
            sem((2, 2)),
            sem((2, 2)),
            sem((2, 8)),
            sem((2, 8)),
            sem((2, 2)),
            sem((2, 2)),
            sem((3, 8)),
            sem((3, 8)),
            sem((2, 8)),
            sem((2, 8)),
            sem((2, 3, 2, 3)),
            sem((2, 3, 2, 3)),
        ],
        compiler_params=pltpu.CompilerParams(
            collective_id=0, has_side_effects=True, vmem_limit_bytes=60 << 20
        ),
        cost_estimate=pl.CostEstimate(
            flops=14 << 30, bytes_accessed=24 << 20, transcendentals=1 << 20
        ),
        name="classify",
    )(
        spectra,
        jnp.asarray(shift_table()),
        offsets.T,
        groups.reshape(1, -1),
        ctf,
        noise_weight.reshape(1, -1),
        references,
        jnp.asarray(harmonic_rows()),
    )
    sums, prob = pl.pallas_call(
        write,
        out_shape=(
            jax.ShapeDtypeStruct((16, 2048), F32),
            jax.ShapeDtypeStruct((1, IMG), F32),
        ),
        in_specs=[vmem, vmem],
        out_specs=(vmem, vmem),
        name="write",
    )(sums, prob)
    return sums, prob.reshape(-1)


def solution(mesh):
    placed = (
        P(("img", "cls"), None, None),
        P(("img", "cls"), None),
        P(("img", "cls")),
        P(),
        P(),
        P("cls", None),
    )
    return jax.shard_map(
        on_device,
        mesh=mesh,
        in_specs=placed,
        out_specs=(P("cls", "img"), P(("img", "cls"))),
        check_vma=False,
    )
```

```python
import math

import jax
import jax.numpy as jnp
import ml_dtypes
import numpy as np
from jax import lax
from jax.experimental import pallas as pl
from jax.experimental.pallas import tpu as pltpu
from jax.sharding import PartitionSpec as P

MESH = pl.DeviceIdType.MESH
F32 = jnp.float32
BF16 = jnp.bfloat16
HIGHEST = lax.Precision.HIGHEST

IMG = 256
R = 64
A = 128
ROTS = 16
SHIFTS = 13
KINDS = (SHIFTS * SHIFTS + 1) // 2
LOW = 88
DEPTH = 176
WX, WY, WZ = 384, 256, 384

SETTLE, FINISH = 2, 5

S1 = math.sqrt(0.5)
C1 = math.cos(math.pi / 8)
C3 = math.cos(3 * math.pi / 8)


def split_np(values):
    high = values.astype(np.float32).astype(ml_dtypes.bfloat16)
    low = (values - high.astype(np.float64)).astype(np.float32).astype(ml_dtypes.bfloat16)
    return high, low


def shift_table():
    theta = 2.0 * np.pi * np.arange(A) / A
    radius = np.arange(R) + 1.0
    step = np.arange(SHIFTS) - 6.0
    along = (
        np.cos(theta)[None, None, :] * step[:, None, None]
        + np.sin(theta)[None, None, :] * step[None, :, None]
    ).reshape(SHIFTS * SHIFTS, A)[:KINDS]
    phase = -2.0 * np.pi * radius[:, None, None] * along[None] / (2.0 * R)
    both = np.concatenate([np.cos(phase), np.sin(phase)], axis=-1)
    high, low = split_np(both)
    table = np.zeros((R, DEPTH, 2 * A), ml_dtypes.bfloat16)
    table[:, :KINDS] = high
    table[:, LOW : LOW + KINDS] = low
    return table


def harmonic_rows():
    quarter = A // ROTS
    orders = ROTS * np.arange(quarter)[None, :] + np.arange(ROTS)[:, None]
    turns = (np.arange(A)[:, None, None] * orders[None]) % A
    angle = 2.0 * np.pi * turns / A
    upper = np.stack([np.cos(angle), -np.sin(angle)], axis=2)
    lower = np.stack([np.sin(angle), np.cos(angle)], axis=2)
    table = np.concatenate([upper, lower], axis=0) / math.sqrt(A)
    return np.ascontiguousarray(table.reshape(2 * A, 2 * A).T).astype(np.float32).astype(
        ml_dtypes.bfloat16
    )


def cosine_part(a):
    p, m = a[0] + a[8], a[0] - a[8]
    t, d = a[2] + a[6], S1 * (a[2] - a[6])
    q = p + a[4]
    even = [q + t, m + d, p - a[4], m - d, q - t]
    s17, d17 = a[1] + a[7], a[1] - a[7]
    s35, d35 = a[3] + a[5], a[3] - a[5]
    odd = [s17 + s35, C1 * d17 + C3 * d35, S1 * (s17 - s35), C3 * d17 - C1 * d35]
    out = [even[k] + odd[k] for k in range(4)] + [even[4]]
    return out + [even[k] - odd[k] for k in (3, 2, 1, 0)]


def sine_part(b):
    t = S1 * (b[2] + b[6])
    even = [None, t + b[4], b[2] - b[6], t - b[4]]
    s17, d17 = b[1] + b[7], b[1] - b[7]
    s35, d35 = b[3] + b[5], b[3] - b[5]
    odd = [None, C3 * s17 + C1 * s35, S1 * (d17 + d35), C1 * s17 - C3 * s35, d17 - d35]
    out = [None] + [odd[k] + even[k] for k in (1, 2, 3)] + [odd[4]]
    return out + [odd[k] - even[k] for k in (3, 2, 1)]


def across(a, b, precision=None):
    return lax.dot_general(
        a, b, (((1,), (1,)), ((), ())), precision=precision, preferred_element_type=F32
    )


def plain(a, b, precision=None):
    return jnp.dot(a, b, precision=precision, preferred_element_type=F32)


def kernel(
    spectra, table, offsets, groups, ctf, noise, refs, harmonics,
    sums_out, prob_out,
    gx, gy, gz, gt, cx, cy, cz, ht, qb, wb, norm, spec, tab, moved, hot, sign, cgt,
    qx, qz, rx1, ry1, rz1, rx2, ry2, rz2, rx3, ry3, rz3,
    dma, ag_s, ag_r, core_s, core_r, qx_s, qx_r, qz_s, qz_r,
    x1_s, x1_r, y1_s, y1_r, z1_s, z1_r, late_s, late_r,
):
    img = lax.axis_index("img")
    cls = lax.axis_index("cls")
    zl, x = img // 4, img % 4
    zh, y, e = cls // 8, (cls // 2) % 4, cls % 2
    other = 1 - e

    def device(zl_, x_, zh_, y_, e_):
        return (zl_ * 4 + x_, zh_ * 8 + y_ * 2 + e_)

    def at_x(d):
        return device(zl, (x + d) % 4, zh, y, e)

    def at_y(d):
        return device(zl, x, zh, (y + d) % 4, e)

    def flip(d):
        return (zh + d // 2) % 2, (zl + d) % 2

    def at_z(d):
        zh_, zl_ = flip(d)
        return device(zl_, x, zh_, y, e)

    twin = device(zl, x, zh, y, other)

    def remote(src, dst, send, recv, where):
        return pltpu.make_async_remote_copy(
            src_ref=src, dst_ref=dst, send_sem=send, recv_sem=recv,
            device_id=where, device_id_type=MESH,
        )

    def spec_copy(c):
        return pltpu.make_async_copy(
            spectra.at[:, pl.ds(c * 16, 16), :], spec.at[c % 2], dma.at[c % 2]
        )

    def tab_copy(c):
        return pltpu.make_async_copy(
            table.at[pl.ds(c * 16, 16)], tab.at[c % 2], dma.at[2 + c % 2]
        )

    barrier = pltpu.get_barrier_semaphore()
    friends = [twin]
    friends += [at_x(d) for d in (1, 2, 3)]
    friends += [at_y(d) for d in (1, 2, 3)]
    friends += [at_z(d) for d in (1, 2, 3)]
    for friend in friends:
        pl.semaphore_signal(barrier, inc=1, device_id=friend, device_id_type=MESH)
    spec_copy(0).start()
    tab_copy(0).start()

    spread = (
        lax.broadcasted_iota(jnp.int32, (R, 512), 0)
        == lax.broadcasted_iota(jnp.int32, (R, 512), 1) // 8
    ).astype(F32)
    nw = jnp.broadcast_to(noise[...], (8, R))
    nwx = plain(nw, spread, HIGHEST)[0:1]

    def weighted(j, first, width, gains):
        start = j * 1024 + first
        part = refs[:, pl.ds(pl.multiple_of(start, 128), width)].astype(F32)
        return (part * gains).astype(BF16)

    gain_x = nwx[:, :384]
    gain_y = jnp.concatenate([nwx[:, 384:], nwx[:, :128]], axis=1)
    gain_z = nwx[:, 128:]
    for h in range(2):
        for k in range(2):
            gx[e, zh, y, x, h, k] = weighted(k * 8 + x * 2 + h, 0, WX, gain_x)
        for k in range(4):
            gz[e, zh, y, zl, h, k] = weighted(zl * 8 + k * 2 + h, WX + WY, WZ, gain_z)
        for k in range(8):
            gy[e, zh, y, h, k // 2, k % 2] = weighted(
                (k % 2) * 8 + (k // 2) * 2 + h, WX, WY, gain_y
            )

    def ag(h, index, piece, where):
        return remote(piece, piece, ag_s.at[h, index], ag_r.at[h, index], where)

    def flip_x(h):
        return ag(h, 3, gx.at[e, zh, y, x, h], at_z(3))

    def pre_x(h):
        return [ag(h, d - 1, gx.at[e, :, y, x, h], at_y(d)) for d in (1, 3, 2)]

    def pre_z(h):
        return [ag(h, 6 + d, gz.at[e, zh, y, zl, h], at_y(d)) for d in (1, 3, 2)]

    def pre_y(h):
        return [ag(h, 10, gy.at[e, zh, y, h], at_z(3))]

    pre_t = ag(0, 32, gt.at[e, zh, y], at_z(3))

    def piece_x(h, e_, d):
        return gx.at[e_, :, :, (x + d) % 4, h]

    def piece_y(h, e_, d):
        return gy.at[e_, :, (y + d) % 4, h]

    def piece_z(h, e_, d):
        zh_, zl_ = flip(d)
        return gz.at[e_, zh_, :, zl_, h]

    def last_x(h, d):
        return ag(h, 10 + d, piece_x(h, e, 0), at_x(d))

    def last_y(h, d):
        return ag(h, 13 + d, piece_y(h, e, 0), at_y(d))

    def last_z(h, d):
        return ag(h, 16 + d, piece_z(h, e, 0), at_z(d))

    def relays(h):
        z_1, z_3 = flip(1), flip(3)
        return [
            ag(h, 4, gx.at[e, 0, :, (x + 3) % 4, h], at_x(1)),
            ag(h, 5, gx.at[e, 1, :, (x + 1) % 4, h], at_x(3)),
            ag(h, 6, gy.at[e, 0, (y + 3) % 4, h], at_y(1)),
            ag(h, 12, gy.at[e, 1, (y + 1) % 4, h], at_y(3)),
            ag(h, 15, gz.at[e, z_3[0], pl.ds(0, 2), z_3[1], h], at_z(1)),
            ag(h, 18, gz.at[e, z_1[0], pl.ds(2, 2), z_1[1], h], at_z(3)),
        ]

    def last_t(d):
        return ag(0, 32 + d, gt.at[e, :, y], at_y(d))

    pieces = (piece_x, piece_y, piece_z)
    lasts = (last_x, last_y, last_z)

    def share(h, group, d):
        return ag(h, 20 + 4 * group + d, pieces[group](h, e, d), twin)

    def share_t(d):
        return ag(0, 36 + d, gt.at[e, :, (y + d) % 4], twin)

    pl.semaphore_wait(barrier, len(friends))
    flip_x(0).start()
    flip_x(1).start()
    for h in range(2):
        for copy in pre_z(h) + pre_y(h):
            copy.start()
        flip_x(h).wait_recv()
        for copy in pre_x(h):
            copy.start()

    total = jnp.zeros((16, 512), F32)
    for k in range(32):
        part = refs[:, k * 512 : (k + 1) * 512].astype(F32)
        total = total + part * part
    ctf4 = jnp.concatenate([ctf[...]] * 4, axis=0)
    by_group = plain(0.5 * noise[...] * ctf4 * ctf4, spread, HIGHEST)
    energy = across(total, by_group, HIGHEST)
    high = energy.astype(BF16).astype(F32)
    middle = (energy - high).astype(BF16).astype(F32)
    low = energy - high - middle
    lane = lax.broadcasted_iota(jnp.int32, (16, 128), 1) // 32
    gt[e, zh, y] = jnp.where(
        lane == 0, high, jnp.where(lane == 1, middle, jnp.where(lane == 2, low, 0.0))
    ).astype(BF16)
    pre_t.start()

    index = (offsets[0:1, :] + 6) * SHIFTS + offsets[1:2, :] + 6
    index = jnp.transpose(jnp.broadcast_to(index.astype(F32), (128, IMG)))
    upper = SHIFTS * SHIFTS - 1.0
    sign[...] = jnp.where(index < KINDS, 1.0, -1.0)
    kind = jnp.minimum(index, upper - index)[:, 0:1]
    column = lax.broadcasted_iota(jnp.int32, (IMG, DEPTH), 1).astype(F32)
    hot[...] = ((column == kind) | (column == kind + LOW)).astype(F32).astype(BF16)
    of_group = (
        lax.broadcasted_iota(jnp.int32, (32, IMG), 0) == groups[...]
    ).astype(F32)
    cgt[...] = lax.dot_general(
        ctf[...], of_group, (((0,), (0,)), ((), ())), precision=HIGHEST, preferred_element_type=F32
    )

    def prepare(c):
        slot = c % 2
        if c < 3:
            spec_copy(c + 1).start()
            tab_copy(c + 1).start()
        spec_copy(c).wait()
        tab_copy(c).wait()

        @pl.loop(0, 16)
        def widen(b):
            part = spec[slot, pl.ds(b * 16, 16)].astype(F32)
            rows = pl.ds(pl.multiple_of(b * 256, 256), 256)
            qb[rows, :] = part[:, :, :A].reshape(256, A)
            rows = pl.ds(pl.multiple_of(4096 + b * 256, 256), 256)
            qb[rows, :] = part[:, :, A:].reshape(256, A)

        @pl.loop(0, 2)
        def move(b):
            for k in range(8):
                r = b * 8 + k
                turn = plain(hot[...], tab[slot, r])
                cosine, sine = turn[:, :A], turn[:, A:] * sign[...]
                real = qb[pl.ds(r, IMG, stride=16), :]
                imag = qb[pl.ds(4096 + r, IMG, stride=16), :]
                moved[r] = jnp.concatenate(
                    [real * cosine - imag * sine, real * sine + imag * cosine], axis=1
                ).astype(BF16)

        @pl.loop(0, 2)
        def transform(b):
            found = []
            for k in range(8):
                r = b * 8 + k
                out = across(harmonics[...], moved[r]) * cgt[pl.ds(c * 16 + r, 1), :]
                found.append(out.reshape(32, 8, IMG))
            both = jnp.concatenate(found, axis=1)
            ht[:, pl.ds(pl.multiple_of(c * 128 + b * 64, 64), 64), :] = both.astype(BF16)

    def pass_on(h):
        for copy in pre_x(h):
            copy.wait_recv()
        for d in (1, 3):
            last_x(h, d).start()
        for copy in pre_z(h) + pre_y(h):
            copy.wait_recv()
        for d in (1, 3):
            last_z(h, d).start()
            last_y(h, d).start()
        if h == 0:
            pre_t.wait_recv()
            for d in (1, 3, 2):
                last_t(d).start()
            share_t(0).start()
        for group in range(3):
            share(h, group, 0).start()

    def relay(h):
        moves = relays(h)
        for k, (group, d) in enumerate(((0, 1), (0, 3), (1, 1), (1, 3), (2, 3), (2, 1))):
            lasts[group](h, d).wait_recv()
            moves[k].start()
            share(h, group, d if group == 2 else 4 - d).start()

    def hand_over(h):
        moves = relays(h)
        for group in range(3):
            moves[2 * group].wait_recv()
            moves[2 * group + 1].wait_recv()
            share(h, group, 2).start()
        if h == 0:
            for d in (1, 3, 2):
                last_t(d).wait_recv()
                share_t(4 - d).start()
        for d in (0, 1, 3, 2):
            for group in range(3):
                share(h, group, d).wait_recv()
            if h == 0:
                share_t(d).wait_recv()

    def correlate(h):
        @pl.loop(0, 4)
        def _(k):
            for zv in range(2):
                j = zv * 8 + k * 2 + h
                part_x = gx[:, :, :, k, h, zv].reshape(256, WX)
                part_y = gy[:, :, :, h, k, zv].reshape(256, WY)
                part_z = gz[:, :, :, zv, h, k].reshape(256, WZ)
                real = jnp.concatenate([part_x, part_y[:, :128]], axis=1)
                imag = jnp.concatenate([part_y[:, 128:], part_z], axis=1)
                h_re, h_im = ht[2 * j], ht[2 * j + 1]
                q_re = plain(real, h_re) + plain(imag, h_im)
                q_im = plain(imag, h_re) - plain(real, h_im)
                for t in range(2):
                    base = pl.multiple_of((t * 32 + 2 * j) * 256, 256)
                    qb[pl.ds(base, 256), :] = q_re[:, t * 128 : (t + 1) * 128]
                    qb[pl.ds(base + 256, 256), :] = q_im[:, t * 128 : (t + 1) * 128]

    prepare(0)
    pass_on(0)
    prepare(1)
    pass_on(1)
    prepare(2)
    relay(0)
    prepare(3)
    relay(1)
    hand_over(0)
    correlate(0)
    hand_over(1)
    correlate(1)

    row = lax.broadcasted_iota(jnp.int32, (128, IMG), 0)
    thrice = ((row % 32 == groups[...]) & (row < 96)).astype(F32).astype(BF16)
    norms = plain(gt[...].reshape(256, 128), thrice)
    norm[0:256, :] = norms[:, :128]
    norm[256:512, :] = norms[:, 128:]

    for t in range(2):
        def at(k, c, t=t):
            return (t * 32 + k) * 256 + c

        def scores(b, top, t=t, at=at):
            c = pl.multiple_of(b * 8, 8)
            re = [qb[pl.ds(at(2 * j, c), 8), :] for j in range(16)]
            im = [qb[pl.ds(at(2 * j + 1, c), 8), :] for j in range(16)]
            a = [re[0]] + [re[j] + re[16 - j] for j in range(1, 8)] + [re[8]]
            s = [None] + [im[j] - im[16 - j] for j in range(1, 8)]
            a[0] = a[0] - norm[pl.ds(t * 256 + c, 8), :]
            cp, sp = cosine_part(a), sine_part(s)
            out = [cp[0]] + [cp[k] + sp[k] for k in range(1, 8)] + [cp[8]]
            out += [cp[16 - k] - sp[16 - k] for k in range(9, 16)]
            for k in range(16):
                qb[pl.ds(at(k, c), 8), :] = out[k]
                top = jnp.maximum(top, out[k])
            return top

        top = lax.fori_loop(0, 32, scores, jnp.full((8, 128), -jnp.inf, F32), unroll=4)
        top = jnp.max(top, axis=0, keepdims=True)

        def exponents(b, total, top=top, at=at):
            c = pl.multiple_of(b * 8, 8)
            for k in range(16):
                value = jnp.exp(qb[pl.ds(at(k, c), 8), :] - top)
                qb[pl.ds(at(k, c), 8), :] = value
                total = total + value
            return total

        total = lax.fori_loop(0, 32, exponents, jnp.zeros((8, 128), F32), unroll=8)
        scale = 1.0 / jnp.sum(total, axis=0, keepdims=True)
        prob_out[:, t * 128 : (t + 1) * 128] = scale

        @pl.loop(0, 16, unroll=2)
        def back(b, t=t, at=at, scale=scale):
            c = pl.multiple_of(b * 16, 16)
            p = [qb[pl.ds(at(k, c), 16), :] * scale for k in range(16)]
            a = [p[0]] + [p[k] + p[16 - k] for k in range(1, 8)] + [p[8]]
            s = [None] + [p[k] - p[16 - k] for k in range(1, 8)]
            cp, sp = cosine_part(a), sine_part(s)
            cols = slice(t * 128, (t + 1) * 128)
            zero = jnp.zeros((16, 128), BF16)
            for j in range(9):
                re = cp[j].astype(BF16)
                wb[j, 0, pl.ds(c, 16), cols] = re
                if j in (0, 8):
                    wb[j, 1, pl.ds(c, 16), cols] = zero
                else:
                    wb[16 - j, 0, pl.ds(c, 16), cols] = re
                    wb[j, 1, pl.ds(c, 16), cols] = sp[j].astype(BF16)
                    wb[16 - j, 1, pl.ds(c, 16), cols] = (-sp[j]).astype(BF16)

    for h in range(2):
        for copy in [flip_x(h)] + pre_x(h) + pre_y(h) + pre_z(h) + relays(h):
            copy.wait_send()
        for group in range(3):
            for d in (1, 3):
                lasts[group](h, d).wait_send()
            for d in range(4):
                share(h, group, d).wait_send()
    pre_t.wait_send()
    for d in (1, 2, 3):
        last_t(d).wait_send()
    for d in range(4):
        share_t(d).wait_send()

    def choose(it, values):
        out = values[0]
        for k in range(1, 8):
            out = jnp.where(it == k, values[k], out)
        return out

    def step_of(it):
        return choose(it, (2, 1, 3, 2, 0, 1, 3, 0)), choose(it, (0, 0, 0, 1, 0, 1, 1, 1))

    def target(it):
        step, h = step_of(it)
        return (x + step) % 4, h

    def trade(it):
        xt, h = target(it)
        pairs = (
            (gx.at[other, :, :, xt, h], cx.at[:, :, xt, h]),
            (gy.at[other, :, :, h, xt], cy.at[:, :, h, xt]),
            (gz.at[other, :, :, :, h, xt], cz.at[:, :, :, h, xt]),
        )
        return [
            remote(src, dst, core_s.at[k, it], core_r.at[k, it], twin)
            for k, (src, dst) in enumerate(pairs)
        ]

    def half_x(h, k):
        return remote(
            gx.at[e, k, :, (x + 2) % 4, h], qx.at[k, h], qx_s.at[k, h], qx_r.at[k, h],
            at_x(1 + 2 * k),
        )

    def half_z(it, k):
        xt, h = target(it)
        zh_, zl_ = flip(2)
        return remote(
            gz.at[e, zh_, pl.ds(2 * k, 2), zl_, h, xt], qz.at[k, it],
            qz_s.at[k, it], qz_r.at[k, it], at_z(1 + 2 * k),
        )

    def first_x(h, k):
        return remote(
            gx.at[e, :, :, (x + 1 + 2 * k) % 4, h], rx1.at[k, h],
            x1_s.at[k, h], x1_r.at[k, h], at_x(1 + 2 * k),
        )

    def first_y(it, d):
        xt, h = target(it)
        return remote(
            gy.at[e, :, (y + d) % 4, h, xt], ry1.at[d - 1, h, :, xt],
            y1_s.at[d - 1, it], y1_r.at[d - 1, it], at_y(d),
        )

    def first_z(it, k):
        xt, h = target(it)
        zh_, zl_ = flip(1 + 2 * k)
        return remote(
            gz.at[e, zh_, :, zl_, h, xt], rz1.at[k, h, :, xt],
            z1_s.at[k, it], z1_r.at[k, it], at_z(1 + 2 * k),
        )

    def settle(it):
        xt, h = target(it)
        for copy in trade(it):
            copy.wait_recv()

        @pl.loop(0, 8)
        def add(s):
            w, v = s // 4, s % 4
            gx[e, w, v, xt, h] = (
                gx[e, w, v, xt, h].astype(F32) + cx[w, v, xt, h].astype(F32)
            ).astype(BF16)
            gy[e, w, v, h, xt] = (
                gy[e, w, v, h, xt].astype(F32) + cy[w, v, h, xt].astype(F32)
            ).astype(BF16)
            gz[e, w, v, :, h, xt] = (
                gz[e, w, v, :, h, xt].astype(F32) + cz[w, v, :, h, xt].astype(F32)
            ).astype(BF16)

        @pl.when((it == 0) | (it == 3))
        def _():
            half_x(h, 0).start()
            half_x(h, 1).start()

        for k in range(2):
            half_z(it, k).start()
        for d in (1, 3, 2):
            first_y(it, d).start()

    def finish(it):
        xt, h = target(it)
        for k in range(2):
            @pl.when((it == 1 + k) | (it == 5 + k))
            def _(k=k):
                half_x(h, k).wait_recv()
                gx[e, k, :, xt, h] = (
                    gx[e, k, :, xt, h].astype(F32) + qx[k, h].astype(F32)
                ).astype(BF16)
                first_x(h, k).start()

        for k in range(2):
            half_z(it, k).wait_recv()
            zh_, zl_ = flip(3 - 2 * k)
            at = pl.ds(2 * k, 2)
            gz[e, zh_, at, zl_, h, xt] = (
                gz[e, zh_, at, zl_, h, xt].astype(F32) + qz[k, it].astype(F32)
            ).astype(BF16)
            first_z(it, 1 - k).start()

    def accumulate(it):
        xt, h = target(it)
        for zv in range(2):
            j = zv * 8 + xt * 2 + h
            w_re, w_im = wb[j, 0], wb[j, 1]
            w_minus = wb[(16 - j) % 16, 1]
            h_both = jnp.concatenate([ht[2 * j], ht[2 * j + 1]], axis=1)
            out_re = across(jnp.concatenate([w_re, w_minus], axis=1), h_both).astype(BF16)
            out_im = across(jnp.concatenate([w_im, w_re], axis=1), h_both).astype(BF16)
            gx[:, :, :, xt, h, zv] = out_re[:, :384].reshape(2, 2, 4, 16, WX)
            gy[:, :, :, h, xt, zv] = jnp.concatenate(
                [out_re[:, 384:], out_im[:, :128]], axis=1
            ).reshape(2, 2, 4, 16, WY)
            gz[:, :, :, zv, h, xt] = out_im[:, 128:].reshape(2, 2, 4, 16, WZ)
        for copy in trade(it):
            copy.start()

    @pl.loop(0, 8 + FINISH)
    def steps(it):
        @pl.when(it < 8)
        def _():
            accumulate(it)

        @pl.when((it >= SETTLE) & (it < 8 + SETTLE))
        def _():
            settle(it - SETTLE)

        @pl.when(it >= FINISH)
        def _():
            finish(it - FINISH)

    def late(stage, group, h, d, src, dst, where):
        return remote(
            src, dst.at[d - 1, h], late_s.at[stage, group, h, d - 1],
            late_r.at[stage, group, h, d - 1], where,
        )

    def second_x(h, d):
        return late(0, 0, h, d, gx.at[e, :, (y + d) % 4, x, h], rx2, at_y(d))

    def second_y(h, d):
        zh_, zl_ = flip(d)
        return late(0, 1, h, d, gy.at[e, zh_, y, h, :, zl_], ry2, at_z(d))

    def second_z(h, d):
        return late(0, 2, h, d, gz.at[e, zh, :, zl, h, (x + d) % 4], rz2, at_x(d))

    def third_x(h, d):
        zh_, zl_ = flip(d)
        return late(1, 0, h, d, gx.at[e, zh_, y, x, h, zl_], rx3, at_z(d))

    def third_y(h, d):
        return late(1, 1, h, d, gy.at[e, zh, y, h, (x + d) % 4, zl], ry3, at_x(d))

    def third_z(h, d):
        return late(1, 2, h, d, gz.at[e, zh, (y + d) % 4, zl, h, x], rz3, at_y(d))

    def total_of(own, parts):
        acc = own.astype(F32)
        for part in parts:
            acc = acc + part.astype(F32)
        return acc

    for h in range(2):
        for k in range(2):
            first_x(h, k).wait_recv()

        @pl.loop(0, 8)
        def add_x1(s, h=h):
            w, v = s // 4, s % 4
            gx[e, w, v, x, h] = total_of(
                gx[e, w, v, x, h], [rx1[k, h, w, v] for k in range(2)]
            ).astype(BF16)

        for d in (1, 3, 2):
            second_x(h, d).start()
        for it in ((0, 1, 2, 4), (3, 5, 6, 7))[h]:
            for k in range(2):
                first_z(it, k).wait_recv()

        @pl.loop(0, 4)
        def add_z1(v, h=h):
            gz[e, zh, v, zl, h] = total_of(
                gz[e, zh, v, zl, h], [rz1[k, h, v] for k in range(2)]
            ).astype(BF16)

        for d in (1, 3, 2):
            second_z(h, d).start()
        for it in ((0, 1, 2, 4), (3, 5, 6, 7))[h]:
            for d in (1, 2, 3):
                first_y(it, d).wait_recv()

        @pl.loop(0, 8)
        def add_y1(s, h=h):
            w, v = s // 4, s % 4
            gy[e, w, y, h, v] = total_of(
                gy[e, w, y, h, v], [ry1[d, h, w, v] for d in range(3)]
            ).astype(BF16)

        for d in (1, 3, 2):
            second_y(h, d).start()

    for h in range(2):
        for d in (1, 3, 2):
            second_x(h, d).wait_recv()
        gx[e, :, y, x, h] = total_of(
            gx[e, :, y, x, h], [rx2[d, h] for d in range(3)]
        ).astype(BF16)
        for d in (1, 3, 2):
            third_x(h, d).start()
        for d in (1, 3, 2):
            second_z(h, d).wait_recv()
        gz[e, zh, :, zl, h, x] = total_of(
            gz[e, zh, :, zl, h, x], [rz2[d, h] for d in range(3)]
        ).astype(BF16)
        for d in (1, 3, 2):
            third_z(h, d).start()
        for d in (1, 3, 2):
            second_y(h, d).wait_recv()
        gy[e, zh, y, h, :, zl] = total_of(
            gy[e, zh, y, h, :, zl], [ry2[d, h] for d in range(3)]
        ).astype(BF16)
        for d in (1, 3, 2):
            third_y(h, d).start()

    for h in range(2):
        first = h * 1024
        for third in (third_x, third_z, third_y):
            for d in (1, 2, 3):
                third(h, d).wait_recv()
        sums_out[:, first : first + WX] = total_of(
            gx[e, zh, y, x, h, zl], [rx3[d, h] for d in range(3)]
        )
        sums_out[:, first + WX : first + WX + WY] = total_of(
            gy[e, zh, y, h, x, zl], [ry3[d, h] for d in range(3)]
        )
        sums_out[:, first + WX + WY : first + 1024] = total_of(
            gz[e, zh, y, zl, h, x], [rz3[d, h] for d in range(3)]
        )

    for it in range(8):
        for copy in trade(it):
            copy.wait_send()
        for k in range(2):
            half_z(it, k).wait_send()
            first_z(it, k).wait_send()
        for d in (1, 2, 3):
            first_y(it, d).wait_send()
    for h in range(2):
        for k in range(2):
            half_x(h, k).wait_send()
            first_x(h, k).wait_send()
    for copy in (second_x, second_y, second_z, third_x, third_y, third_z):
        for h in range(2):
            for d in (1, 2, 3):
                copy(h, d).wait_send()


def write(sums, prob, sums_out, prob_out):
    sums_out[...] = sums[...]
    prob_out[...] = prob[...]


def on_device(spectra, offsets, groups, ctf, noise_weight, references):
    vmem = pl.BlockSpec(memory_space=pltpu.VMEM)
    anywhere = pl.BlockSpec(memory_space=pl.ANY)
    sem = pltpu.SemaphoreType.DMA
    sums, prob = pl.pallas_call(
        kernel,
        out_shape=(
            jax.ShapeDtypeStruct((16, 2048), F32),
            jax.ShapeDtypeStruct((1, IMG), F32),
        ),
        in_specs=[anywhere, anywhere] + [vmem] * 6,
        out_specs=(vmem, vmem),
        scratch_shapes=[
            pltpu.VMEM((2, 2, 4, 4, 2, 2, 16, WX), BF16),
            pltpu.VMEM((2, 2, 4, 2, 4, 2, 16, WY), BF16),
            pltpu.VMEM((2, 2, 4, 2, 2, 4, 16, WZ), BF16),
            pltpu.VMEM((2, 2, 4, 16, 128), BF16),
            pltpu.VMEM((2, 4, 4, 2, 2, 16, WX), BF16),
            pltpu.VMEM((2, 4, 2, 4, 2, 16, WY), BF16),
            pltpu.VMEM((2, 4, 2, 2, 4, 16, WZ), BF16),
            pltpu.VMEM((32, 512, IMG), BF16),
            pltpu.VMEM((16384, 128), F32),
            pltpu.VMEM((16, 2, 256, IMG), BF16),
            pltpu.VMEM((512, 128), F32),
            pltpu.VMEM((2, IMG, 16, 2 * A), BF16),
            pltpu.VMEM((2, 16, DEPTH, 2 * A), BF16),
            pltpu.VMEM((16, IMG, 2 * A), BF16),
            pltpu.VMEM((IMG, DEPTH), BF16),
            pltpu.VMEM((IMG, A), F32),
            pltpu.VMEM((R, IMG), F32),
            pltpu.VMEM((2, 2, 4, 2, 16, WX), BF16),
            pltpu.VMEM((2, 8, 2, 16, WZ), BF16),
            pltpu.VMEM((2, 2, 2, 4, 2, 16, WX), BF16),
            pltpu.VMEM((3, 2, 2, 4, 2, 16, WY), BF16),
            pltpu.VMEM((2, 2, 4, 4, 16, WZ), BF16),
            pltpu.VMEM((3, 2, 2, 2, 16, WX), BF16),
            pltpu.VMEM((3, 2, 4, 16, WY), BF16),
            pltpu.VMEM((3, 2, 4, 16, WZ), BF16),
            pltpu.VMEM((3, 2, 16, WX), BF16),
            pltpu.VMEM((3, 2, 16, WY), BF16),
            pltpu.VMEM((3, 2, 16, WZ), BF16),
            sem((4,)),
            sem((2, 40)),
            sem((2, 40)),
            sem((3, 8)),
            sem((3, 8)),
            sem((2, 2)),
            sem((2, 2)),
            sem((2, 8)),
            sem((2, 8)),
            sem((2, 2)),
            sem((2, 2)),
            sem((3, 8)),
            sem((3, 8)),
            sem((2, 8)),
            sem((2, 8)),
            sem((2, 3, 2, 3)),
            sem((2, 3, 2, 3)),
        ],
        compiler_params=pltpu.CompilerParams(
            collective_id=0, has_side_effects=True, vmem_limit_bytes=60 << 20
        ),
        cost_estimate=pl.CostEstimate(
            flops=14 << 30, bytes_accessed=24 << 20, transcendentals=1 << 20
        ),
        name="classify",
    )(
        spectra,
        jnp.asarray(shift_table()),
        offsets.T,
        groups.reshape(1, -1),
        ctf,
        noise_weight.reshape(1, -1),
        references,
        jnp.asarray(harmonic_rows()),
    )
    sums, prob = pl.pallas_call(
        write,
        out_shape=(
            jax.ShapeDtypeStruct((16, 2048), F32),
            jax.ShapeDtypeStruct((1, IMG), F32),
        ),
        in_specs=[vmem, vmem],
        out_specs=(vmem, vmem),
        name="write",
    )(sums, prob)
    return sums, prob.reshape(-1)


def solution(mesh):
    placed = (
        P(("img", "cls"), None, None),
        P(("img", "cls"), None),
        P(("img", "cls")),
        P(),
        P(),
        P("cls", None),
    )
    return jax.shard_map(
        on_device,
        mesh=mesh,
        in_specs=placed,
        out_specs=(P("cls", "img"), P(("img", "cls"))),
        check_vma=False,
    )
```

```python
import math

import jax
import jax.numpy as jnp
import ml_dtypes
import numpy as np
from jax import lax
from jax.experimental import pallas as pl
from jax.experimental.pallas import tpu as pltpu
from jax.sharding import PartitionSpec as P

MESH = pl.DeviceIdType.MESH
F32 = jnp.float32
BF16 = jnp.bfloat16
HIGHEST = lax.Precision.HIGHEST

IMG = 256
R = 64
A = 128
ROTS = 16
SHIFTS = 13
KINDS = (SHIFTS * SHIFTS + 1) // 2
LOW = 88
DEPTH = 176
WX, WY, WZ = 384, 256, 384

SETTLE, FINISH = 2, 5

S1 = math.sqrt(0.5)
C1 = math.cos(math.pi / 8)
C3 = math.cos(3 * math.pi / 8)


def split_np(values):
    high = values.astype(np.float32).astype(ml_dtypes.bfloat16)
    low = (values - high.astype(np.float64)).astype(np.float32).astype(ml_dtypes.bfloat16)
    return high, low


def shift_table():
    theta = 2.0 * np.pi * np.arange(A) / A
    radius = np.arange(R) + 1.0
    step = np.arange(SHIFTS) - 6.0
    along = (
        np.cos(theta)[None, None, :] * step[:, None, None]
        + np.sin(theta)[None, None, :] * step[None, :, None]
    ).reshape(SHIFTS * SHIFTS, A)[:KINDS]
    phase = -2.0 * np.pi * radius[:, None, None] * along[None] / (2.0 * R)
    both = np.concatenate([np.cos(phase), np.sin(phase)], axis=-1)
    high, low = split_np(both)
    table = np.zeros((R, DEPTH, 2 * A), ml_dtypes.bfloat16)
    table[:, :KINDS] = high
    table[:, LOW : LOW + KINDS] = low
    return table


def harmonic_rows():
    quarter = A // ROTS
    orders = ROTS * np.arange(quarter)[None, :] + np.arange(ROTS)[:, None]
    turns = (np.arange(A)[:, None, None] * orders[None]) % A
    angle = 2.0 * np.pi * turns / A
    upper = np.stack([np.cos(angle), -np.sin(angle)], axis=2)
    lower = np.stack([np.sin(angle), np.cos(angle)], axis=2)
    table = np.concatenate([upper, lower], axis=0) / math.sqrt(A)
    return np.ascontiguousarray(table.reshape(2 * A, 2 * A).T).astype(np.float32).astype(
        ml_dtypes.bfloat16
    )


def cosine_part(a):
    p, m = a[0] + a[8], a[0] - a[8]
    t, d = a[2] + a[6], S1 * (a[2] - a[6])
    q = p + a[4]
    even = [q + t, m + d, p - a[4], m - d, q - t]
    s17, d17 = a[1] + a[7], a[1] - a[7]
    s35, d35 = a[3] + a[5], a[3] - a[5]
    odd = [s17 + s35, C1 * d17 + C3 * d35, S1 * (s17 - s35), C3 * d17 - C1 * d35]
    out = [even[k] + odd[k] for k in range(4)] + [even[4]]
    return out + [even[k] - odd[k] for k in (3, 2, 1, 0)]


def sine_part(b):
    t = S1 * (b[2] + b[6])
    even = [None, t + b[4], b[2] - b[6], t - b[4]]
    s17, d17 = b[1] + b[7], b[1] - b[7]
    s35, d35 = b[3] + b[5], b[3] - b[5]
    odd = [None, C3 * s17 + C1 * s35, S1 * (d17 + d35), C1 * s17 - C3 * s35, d17 - d35]
    out = [None] + [odd[k] + even[k] for k in (1, 2, 3)] + [odd[4]]
    return out + [odd[k] - even[k] for k in (3, 2, 1)]


def across(a, b, precision=None):
    return lax.dot_general(
        a, b, (((1,), (1,)), ((), ())), precision=precision, preferred_element_type=F32
    )


def plain(a, b, precision=None):
    return jnp.dot(a, b, precision=precision, preferred_element_type=F32)


def kernel(
    spectra, table, offsets, groups, ctf, noise, refs, harmonics,
    sums_out, prob_out,
    gx, gy, gz, gt, cx, cy, cz, ht, qb, wb, norm, spec, tab, moved, hot, sign, cgt,
    qx, qz, rx1, ry1, rz1, rx2, ry2, rz2, rx3, ry3, rz3,
    dma, ag_s, ag_r, core_s, core_r, qx_s, qx_r, qz_s, qz_r,
    x1_s, x1_r, y1_s, y1_r, z1_s, z1_r, late_s, late_r,
):
    img = lax.axis_index("img")
    cls = lax.axis_index("cls")
    zl, x = img // 4, img % 4
    zh, y, e = cls // 8, (cls // 2) % 4, cls % 2
    other = 1 - e

    def device(zl_, x_, zh_, y_, e_):
        return (zl_ * 4 + x_, zh_ * 8 + y_ * 2 + e_)

    def at_x(d):
        return device(zl, (x + d) % 4, zh, y, e)

    def at_y(d):
        return device(zl, x, zh, (y + d) % 4, e)

    def flip(d):
        return (zh + d // 2) % 2, (zl + d) % 2

    def at_z(d):
        zh_, zl_ = flip(d)
        return device(zl_, x, zh_, y, e)

    twin = device(zl, x, zh, y, other)

    def remote(src, dst, send, recv, where):
        return pltpu.make_async_remote_copy(
            src_ref=src, dst_ref=dst, send_sem=send, recv_sem=recv,
            device_id=where, device_id_type=MESH,
        )

    def spec_copy(c):
        return pltpu.make_async_copy(
            spectra.at[:, pl.ds(c * 16, 16), :], spec.at[c % 2], dma.at[c % 2]
        )

    def tab_copy(c):
        return pltpu.make_async_copy(
            table.at[pl.ds(c * 16, 16)], tab.at[c % 2], dma.at[2 + c % 2]
        )

    barrier = pltpu.get_barrier_semaphore()
    friends = [twin]
    friends += [at_x(d) for d in (1, 2, 3)]
    friends += [at_y(d) for d in (1, 2, 3)]
    friends += [at_z(d) for d in (1, 2, 3)]
    for friend in friends:
        pl.semaphore_signal(barrier, inc=1, device_id=friend, device_id_type=MESH)
    spec_copy(0).start()
    tab_copy(0).start()

    spread = (
        lax.broadcasted_iota(jnp.int32, (R, 512), 0)
        == lax.broadcasted_iota(jnp.int32, (R, 512), 1) // 8
    ).astype(F32)
    nw = jnp.broadcast_to(noise[...], (8, R))
    nwx = plain(nw, spread, HIGHEST)[0:1]

    def weighted(j, first, width, gains):
        start = j * 1024 + first
        part = refs[:, pl.ds(pl.multiple_of(start, 128), width)].astype(F32)
        return (part * gains).astype(BF16)

    gain_x = nwx[:, :384]
    gain_y = jnp.concatenate([nwx[:, 384:], nwx[:, :128]], axis=1)
    gain_z = nwx[:, 128:]
    for h in range(2):
        for k in range(2):
            gx[e, zh, y, x, h, k] = weighted(k * 8 + x * 2 + h, 0, WX, gain_x)
        for k in range(4):
            gz[e, zh, y, zl, h, k] = weighted(zl * 8 + k * 2 + h, WX + WY, WZ, gain_z)
        for k in range(8):
            gy[e, zh, y, h, k // 2, k % 2] = weighted(
                (k % 2) * 8 + (k // 2) * 2 + h, WX, WY, gain_y
            )

    def ag(h, index, piece, where):
        return remote(piece, piece, ag_s.at[h, index], ag_r.at[h, index], where)

    def flip_x(h):
        return ag(h, 3, gx.at[e, zh, y, x, h], at_z(3))

    def pre_x(h):
        return [ag(h, d - 1, gx.at[e, :, y, x, h], at_y(d)) for d in (1, 3, 2)]

    def pre_z(h):
        return [ag(h, 6 + d, gz.at[e, zh, y, zl, h], at_y(d)) for d in (1, 3, 2)]

    def pre_y(h):
        return [ag(h, 10, gy.at[e, zh, y, h], at_z(3))]

    pre_t = ag(0, 32, gt.at[e, zh, y], at_z(3))

    def piece_x(h, e_, d):
        return gx.at[e_, :, :, (x + d) % 4, h]

    def piece_y(h, e_, d):
        return gy.at[e_, :, (y + d) % 4, h]

    def piece_z(h, e_, d):
        zh_, zl_ = flip(d)
        return gz.at[e_, zh_, :, zl_, h]

    def last_x(h, d):
        return ag(h, 10 + d, piece_x(h, e, 0), at_x(d))

    def last_y(h, d):
        return ag(h, 13 + d, piece_y(h, e, 0), at_y(d))

    def last_z(h, d):
        return ag(h, 16 + d, piece_z(h, e, 0), at_z(d))

    def relays(h):
        z_1, z_3 = flip(1), flip(3)
        return [
            ag(h, 4, gx.at[e, 0, :, (x + 3) % 4, h], at_x(1)),
            ag(h, 5, gx.at[e, 1, :, (x + 1) % 4, h], at_x(3)),
            ag(h, 6, gy.at[e, 0, (y + 3) % 4, h], at_y(1)),
            ag(h, 12, gy.at[e, 1, (y + 1) % 4, h], at_y(3)),
            ag(h, 15, gz.at[e, z_3[0], pl.ds(0, 2), z_3[1], h], at_z(1)),
            ag(h, 18, gz.at[e, z_1[0], pl.ds(2, 2), z_1[1], h], at_z(3)),
        ]

    def last_t(d):
        return ag(0, 32 + d, gt.at[e, :, y], at_y(d))

    pieces = (piece_x, piece_y, piece_z)
    lasts = (last_x, last_y, last_z)

    def share(h, group, d):
        return ag(h, 20 + 4 * group + d, pieces[group](h, e, d), twin)

    def share_t(d):
        return ag(0, 36 + d, gt.at[e, :, (y + d) % 4], twin)

    pl.semaphore_wait(barrier, len(friends))
    flip_x(0).start()
    flip_x(1).start()
    for h in range(2):
        for copy in pre_z(h) + pre_y(h):
            copy.start()
        flip_x(h).wait_recv()
        for copy in pre_x(h):
            copy.start()

    total = jnp.zeros((16, 512), F32)
    for k in range(32):
        part = refs[:, k * 512 : (k + 1) * 512].astype(F32)
        total = total + part * part
    ctf4 = jnp.concatenate([ctf[...]] * 4, axis=0)
    by_group = plain(0.5 * noise[...] * ctf4 * ctf4, spread, HIGHEST)
    energy = across(total, by_group, HIGHEST)
    high = energy.astype(BF16).astype(F32)
    middle = (energy - high).astype(BF16).astype(F32)
    low = energy - high - middle
    lane = lax.broadcasted_iota(jnp.int32, (16, 128), 1) // 32
    gt[e, zh, y] = jnp.where(
        lane == 0, high, jnp.where(lane == 1, middle, jnp.where(lane == 2, low, 0.0))
    ).astype(BF16)
    pre_t.start()

    index = (offsets[0:1, :] + 6) * SHIFTS + offsets[1:2, :] + 6
    index = jnp.transpose(jnp.broadcast_to(index.astype(F32), (128, IMG)))
    upper = SHIFTS * SHIFTS - 1.0
    sign[...] = jnp.where(index < KINDS, 1.0, -1.0)
    kind = jnp.minimum(index, upper - index)[:, 0:1]
    column = lax.broadcasted_iota(jnp.int32, (IMG, DEPTH), 1).astype(F32)
    hot[...] = ((column == kind) | (column == kind + LOW)).astype(F32).astype(BF16)
    of_group = (
        lax.broadcasted_iota(jnp.int32, (32, IMG), 0) == groups[...]
    ).astype(F32)
    cgt[...] = lax.dot_general(
        ctf[...], of_group, (((0,), (0,)), ((), ())), precision=HIGHEST, preferred_element_type=F32
    )

    def prepare(c):
        slot = c % 2
        if c < 3:
            spec_copy(c + 1).start()
            tab_copy(c + 1).start()
        spec_copy(c).wait()
        tab_copy(c).wait()

        @pl.loop(0, 16)
        def widen(b):
            part = spec[slot, pl.ds(b * 16, 16)].astype(F32)
            rows = pl.ds(pl.multiple_of(b * 256, 256), 256)
            qb[rows, :] = part[:, :, :A].reshape(256, A)
            rows = pl.ds(pl.multiple_of(4096 + b * 256, 256), 256)
            qb[rows, :] = part[:, :, A:].reshape(256, A)

        @pl.loop(0, 2)
        def move(b):
            for k in range(8):
                r = b * 8 + k
                turn = plain(hot[...], tab[slot, r])
                cosine, sine = turn[:, :A], turn[:, A:] * sign[...]
                real = qb[pl.ds(r, IMG, stride=16), :]
                imag = qb[pl.ds(4096 + r, IMG, stride=16), :]
                moved[r] = jnp.concatenate(
                    [real * cosine - imag * sine, real * sine + imag * cosine], axis=1
                ).astype(BF16)

        @pl.loop(0, 2)
        def transform(b):
            found = []
            for k in range(8):
                r = b * 8 + k
                out = across(harmonics[...], moved[r]) * cgt[pl.ds(c * 16 + r, 1), :]
                found.append(out.reshape(32, 8, IMG))
            both = jnp.concatenate(found, axis=1)
            ht[:, pl.ds(pl.multiple_of(c * 128 + b * 64, 64), 64), :] = both.astype(BF16)

    def pass_on(h):
        for copy in pre_x(h):
            copy.wait_recv()
        for d in (1, 3):
            last_x(h, d).start()
        for copy in pre_z(h) + pre_y(h):
            copy.wait_recv()
        for d in (1, 3):
            last_z(h, d).start()
            last_y(h, d).start()
        if h == 0:
            pre_t.wait_recv()
            for d in (1, 3, 2):
                last_t(d).start()
            share_t(0).start()
        for group in range(3):
            share(h, group, 0).start()

    def relay(h):
        moves = relays(h)
        for k, (group, d) in enumerate(((0, 1), (0, 3), (1, 1), (1, 3), (2, 3), (2, 1))):
            lasts[group](h, d).wait_recv()
            moves[k].start()
            share(h, group, d if group == 2 else 4 - d).start()

    def hand_over(h):
        moves = relays(h)
        for group in range(3):
            moves[2 * group].wait_recv()
            moves[2 * group + 1].wait_recv()
            share(h, group, 2).start()
        if h == 0:
            for d in (1, 3, 2):
                last_t(d).wait_recv()
                share_t(4 - d).start()
        for d in (0, 1, 3, 2):
            for group in range(3):
                share(h, group, d).wait_recv()
            if h == 0:
                share_t(d).wait_recv()

    def correlate(h):
        @pl.loop(0, 4, unroll=2)
        def _(k):
            for zv in range(2):
                j = zv * 8 + k * 2 + h
                part_x = gx[:, :, :, k, h, zv].reshape(256, WX)
                part_y = gy[:, :, :, h, k, zv].reshape(256, WY)
                part_z = gz[:, :, :, zv, h, k].reshape(256, WZ)
                real = jnp.concatenate([part_x, part_y[:, :128]], axis=1)
                imag = jnp.concatenate([part_y[:, 128:], part_z], axis=1)
                h_re, h_im = ht[2 * j], ht[2 * j + 1]
                q_re = plain(real, h_re) + plain(imag, h_im)
                q_im = plain(imag, h_re) - plain(real, h_im)
                for t in range(2):
                    base = pl.multiple_of((t * 32 + 2 * j) * 256, 256)
                    qb[pl.ds(base, 256), :] = q_re[:, t * 128 : (t + 1) * 128]
                    qb[pl.ds(base + 256, 256), :] = q_im[:, t * 128 : (t + 1) * 128]

    prepare(0)
    pass_on(0)
    prepare(1)
    pass_on(1)
    prepare(2)
    relay(0)
    prepare(3)
    relay(1)
    hand_over(0)
    correlate(0)
    hand_over(1)
    correlate(1)

    row = lax.broadcasted_iota(jnp.int32, (128, IMG), 0)
    thrice = ((row % 32 == groups[...]) & (row < 96)).astype(F32).astype(BF16)
    norms = plain(gt[...].reshape(256, 128), thrice)
    norm[0:256, :] = norms[:, :128]
    norm[256:512, :] = norms[:, 128:]

    for t in range(2):
        def at(k, c, t=t):
            return (t * 32 + k) * 256 + c

        def scores(b, top, t=t, at=at):
            c = pl.multiple_of(b * 8, 8)
            re = [qb[pl.ds(at(2 * j, c), 8), :] for j in range(16)]
            im = [qb[pl.ds(at(2 * j + 1, c), 8), :] for j in range(16)]
            a = [re[0]] + [re[j] + re[16 - j] for j in range(1, 8)] + [re[8]]
            s = [None] + [im[j] - im[16 - j] for j in range(1, 8)]
            a[0] = a[0] - norm[pl.ds(t * 256 + c, 8), :]
            cp, sp = cosine_part(a), sine_part(s)
            out = [cp[0]] + [cp[k] + sp[k] for k in range(1, 8)] + [cp[8]]
            out += [cp[16 - k] - sp[16 - k] for k in range(9, 16)]
            for k in range(16):
                qb[pl.ds(at(k, c), 8), :] = out[k]
                top = jnp.maximum(top, out[k])
            return top

        top = lax.fori_loop(0, 32, scores, jnp.full((8, 128), -jnp.inf, F32), unroll=4)
        top = jnp.max(top, axis=0, keepdims=True)

        def exponents(b, total, top=top, at=at):
            c = pl.multiple_of(b * 8, 8)
            for k in range(16):
                value = jnp.exp(qb[pl.ds(at(k, c), 8), :] - top)
                qb[pl.ds(at(k, c), 8), :] = value
                total = total + value
            return total

        total = lax.fori_loop(0, 32, exponents, jnp.zeros((8, 128), F32), unroll=8)
        scale = 1.0 / jnp.sum(total, axis=0, keepdims=True)
        prob_out[:, t * 128 : (t + 1) * 128] = scale

        @pl.loop(0, 16, unroll=2)
        def back(b, t=t, at=at, scale=scale):
            c = pl.multiple_of(b * 16, 16)
            p = [qb[pl.ds(at(k, c), 16), :] * scale for k in range(16)]
            a = [p[0]] + [p[k] + p[16 - k] for k in range(1, 8)] + [p[8]]
            s = [None] + [p[k] - p[16 - k] for k in range(1, 8)]
            cp, sp = cosine_part(a), sine_part(s)
            cols = slice(t * 128, (t + 1) * 128)
            zero = jnp.zeros((16, 128), BF16)
            for j in range(9):
                re = cp[j].astype(BF16)
                wb[j, 0, pl.ds(c, 16), cols] = re
                if j in (0, 8):
                    wb[j, 1, pl.ds(c, 16), cols] = zero
                else:
                    wb[16 - j, 0, pl.ds(c, 16), cols] = re
                    wb[j, 1, pl.ds(c, 16), cols] = sp[j].astype(BF16)
                    wb[16 - j, 1, pl.ds(c, 16), cols] = (-sp[j]).astype(BF16)

    for h in range(2):
        for copy in [flip_x(h)] + pre_x(h) + pre_y(h) + pre_z(h) + relays(h):
            copy.wait_send()
        for group in range(3):
            for d in (1, 3):
                lasts[group](h, d).wait_send()
            for d in range(4):
                share(h, group, d).wait_send()
    pre_t.wait_send()
    for d in (1, 2, 3):
        last_t(d).wait_send()
    for d in range(4):
        share_t(d).wait_send()

    def choose(it, values):
        out = values[0]
        for k in range(1, 8):
            out = jnp.where(it == k, values[k], out)
        return out

    def step_of(it):
        return choose(it, (2, 1, 3, 2, 0, 1, 3, 0)), choose(it, (0, 0, 0, 1, 0, 1, 1, 1))

    def target(it):
        step, h = step_of(it)
        return (x + step) % 4, h

    def trade(it):
        xt, h = target(it)
        pairs = (
            (gx.at[other, :, :, xt, h], cx.at[:, :, xt, h]),
            (gy.at[other, :, :, h, xt], cy.at[:, :, h, xt]),
            (gz.at[other, :, :, :, h, xt], cz.at[:, :, :, h, xt]),
        )
        return [
            remote(src, dst, core_s.at[k, it], core_r.at[k, it], twin)
            for k, (src, dst) in enumerate(pairs)
        ]

    def half_x(h, k):
        return remote(
            gx.at[e, k, :, (x + 2) % 4, h], qx.at[k, h], qx_s.at[k, h], qx_r.at[k, h],
            at_x(1 + 2 * k),
        )

    def half_z(it, k):
        xt, h = target(it)
        zh_, zl_ = flip(2)
        return remote(
            gz.at[e, zh_, pl.ds(2 * k, 2), zl_, h, xt], qz.at[k, it],
            qz_s.at[k, it], qz_r.at[k, it], at_z(1 + 2 * k),
        )

    def first_x(h, k):
        return remote(
            gx.at[e, :, :, (x + 1 + 2 * k) % 4, h], rx1.at[k, h],
            x1_s.at[k, h], x1_r.at[k, h], at_x(1 + 2 * k),
        )

    def first_y(it, d):
        xt, h = target(it)
        return remote(
            gy.at[e, :, (y + d) % 4, h, xt], ry1.at[d - 1, h, :, xt],
            y1_s.at[d - 1, it], y1_r.at[d - 1, it], at_y(d),
        )

    def first_z(it, k):
        xt, h = target(it)
        zh_, zl_ = flip(1 + 2 * k)
        return remote(
            gz.at[e, zh_, :, zl_, h, xt], rz1.at[k, h, :, xt],
            z1_s.at[k, it], z1_r.at[k, it], at_z(1 + 2 * k),
        )

    def settle(it):
        xt, h = target(it)
        for copy in trade(it):
            copy.wait_recv()

        @pl.loop(0, 8, unroll=2)
        def add(s):
            w, v = s // 4, s % 4
            gx[e, w, v, xt, h] = (
                gx[e, w, v, xt, h].astype(F32) + cx[w, v, xt, h].astype(F32)
            ).astype(BF16)
            gy[e, w, v, h, xt] = (
                gy[e, w, v, h, xt].astype(F32) + cy[w, v, h, xt].astype(F32)
            ).astype(BF16)
            gz[e, w, v, :, h, xt] = (
                gz[e, w, v, :, h, xt].astype(F32) + cz[w, v, :, h, xt].astype(F32)
            ).astype(BF16)

        @pl.when((it == 0) | (it == 3))
        def _():
            half_x(h, 0).start()
            half_x(h, 1).start()

        for k in range(2):
            half_z(it, k).start()
        for d in (1, 3, 2):
            first_y(it, d).start()

    def finish(it):
        xt, h = target(it)
        for k in range(2):
            @pl.when((it == 1 + k) | (it == 5 + k))
            def _(k=k):
                half_x(h, k).wait_recv()
                gx[e, k, :, xt, h] = (
                    gx[e, k, :, xt, h].astype(F32) + qx[k, h].astype(F32)
                ).astype(BF16)
                first_x(h, k).start()

        for k in range(2):
            half_z(it, k).wait_recv()
            zh_, zl_ = flip(3 - 2 * k)
            at = pl.ds(2 * k, 2)
            gz[e, zh_, at, zl_, h, xt] = (
                gz[e, zh_, at, zl_, h, xt].astype(F32) + qz[k, it].astype(F32)
            ).astype(BF16)
            first_z(it, 1 - k).start()

    def accumulate(it):
        xt, h = target(it)
        for zv in range(2):
            j = zv * 8 + xt * 2 + h
            w_re, w_im = wb[j, 0], wb[j, 1]
            w_minus = wb[(16 - j) % 16, 1]
            h_both = jnp.concatenate([ht[2 * j], ht[2 * j + 1]], axis=1)
            out_re = across(jnp.concatenate([w_re, w_minus], axis=1), h_both).astype(BF16)
            out_im = across(jnp.concatenate([w_im, w_re], axis=1), h_both).astype(BF16)
            gx[:, :, :, xt, h, zv] = out_re[:, :384].reshape(2, 2, 4, 16, WX)
            gy[:, :, :, h, xt, zv] = jnp.concatenate(
                [out_re[:, 384:], out_im[:, :128]], axis=1
            ).reshape(2, 2, 4, 16, WY)
            gz[:, :, :, zv, h, xt] = out_im[:, 128:].reshape(2, 2, 4, 16, WZ)
        for copy in trade(it):
            copy.start()

    @pl.loop(0, 8 + FINISH)
    def steps(it):
        @pl.when(it < 8)
        def _():
            accumulate(it)

        @pl.when((it >= SETTLE) & (it < 8 + SETTLE))
        def _():
            settle(it - SETTLE)

        @pl.when(it >= FINISH)
        def _():
            finish(it - FINISH)

    def late(stage, group, h, d, src, dst, where):
        return remote(
            src, dst.at[d - 1, h], late_s.at[stage, group, h, d - 1],
            late_r.at[stage, group, h, d - 1], where,
        )

    def second_x(h, d):
        return late(0, 0, h, d, gx.at[e, :, (y + d) % 4, x, h], rx2, at_y(d))

    def second_y(h, d):
        zh_, zl_ = flip(d)
        return late(0, 1, h, d, gy.at[e, zh_, y, h, :, zl_], ry2, at_z(d))

    def second_z(h, d):
        return late(0, 2, h, d, gz.at[e, zh, :, zl, h, (x + d) % 4], rz2, at_x(d))

    def third_x(h, d):
        zh_, zl_ = flip(d)
        return late(1, 0, h, d, gx.at[e, zh_, y, x, h, zl_], rx3, at_z(d))

    def third_y(h, d):
        return late(1, 1, h, d, gy.at[e, zh, y, h, (x + d) % 4, zl], ry3, at_x(d))

    def third_z(h, d):
        return late(1, 2, h, d, gz.at[e, zh, (y + d) % 4, zl, h, x], rz3, at_y(d))

    def total_of(own, parts):
        acc = own.astype(F32)
        for part in parts:
            acc = acc + part.astype(F32)
        return acc

    for h in range(2):
        for k in range(2):
            first_x(h, k).wait_recv()

        @pl.loop(0, 8, unroll=4)
        def add_x1(s, h=h):
            w, v = s // 4, s % 4
            gx[e, w, v, x, h] = total_of(
                gx[e, w, v, x, h], [rx1[k, h, w, v] for k in range(2)]
            ).astype(BF16)

        for d in (1, 3, 2):
            second_x(h, d).start()
        for it in ((0, 1, 2, 4), (3, 5, 6, 7))[h]:
            for k in range(2):
                first_z(it, k).wait_recv()

        @pl.loop(0, 4, unroll=4)
        def add_z1(v, h=h):
            gz[e, zh, v, zl, h] = total_of(
                gz[e, zh, v, zl, h], [rz1[k, h, v] for k in range(2)]
            ).astype(BF16)

        for d in (1, 3, 2):
            second_z(h, d).start()
        for it in ((0, 1, 2, 4), (3, 5, 6, 7))[h]:
            for d in (1, 2, 3):
                first_y(it, d).wait_recv()

        @pl.loop(0, 8, unroll=4)
        def add_y1(s, h=h):
            w, v = s // 4, s % 4
            gy[e, w, y, h, v] = total_of(
                gy[e, w, y, h, v], [ry1[d, h, w, v] for d in range(3)]
            ).astype(BF16)

        for d in (1, 3, 2):
            second_y(h, d).start()

    for h in range(2):
        for d in (1, 3, 2):
            second_x(h, d).wait_recv()
        gx[e, :, y, x, h] = total_of(
            gx[e, :, y, x, h], [rx2[d, h] for d in range(3)]
        ).astype(BF16)
        for d in (1, 3, 2):
            third_x(h, d).start()
        for d in (1, 3, 2):
            second_z(h, d).wait_recv()
        gz[e, zh, :, zl, h, x] = total_of(
            gz[e, zh, :, zl, h, x], [rz2[d, h] for d in range(3)]
        ).astype(BF16)
        for d in (1, 3, 2):
            third_z(h, d).start()
        for d in (1, 3, 2):
            second_y(h, d).wait_recv()
        gy[e, zh, y, h, :, zl] = total_of(
            gy[e, zh, y, h, :, zl], [ry2[d, h] for d in range(3)]
        ).astype(BF16)
        for d in (1, 3, 2):
            third_y(h, d).start()

    for h in range(2):
        first = h * 1024
        for third in (third_x, third_z, third_y):
            for d in (1, 2, 3):
                third(h, d).wait_recv()
        sums_out[:, first : first + WX] = total_of(
            gx[e, zh, y, x, h, zl], [rx3[d, h] for d in range(3)]
        )
        sums_out[:, first + WX : first + WX + WY] = total_of(
            gy[e, zh, y, h, x, zl], [ry3[d, h] for d in range(3)]
        )
        sums_out[:, first + WX + WY : first + 1024] = total_of(
            gz[e, zh, y, zl, h, x], [rz3[d, h] for d in range(3)]
        )

    for it in range(8):
        for copy in trade(it):
            copy.wait_send()
        for k in range(2):
            half_z(it, k).wait_send()
            first_z(it, k).wait_send()
        for d in (1, 2, 3):
            first_y(it, d).wait_send()
    for h in range(2):
        for k in range(2):
            half_x(h, k).wait_send()
            first_x(h, k).wait_send()
    for copy in (second_x, second_y, second_z, third_x, third_y, third_z):
        for h in range(2):
            for d in (1, 2, 3):
                copy(h, d).wait_send()


def write(sums, prob, sums_out, prob_out):
    sums_out[...] = sums[...]
    prob_out[...] = prob[...]


def on_device(spectra, offsets, groups, ctf, noise_weight, references):
    vmem = pl.BlockSpec(memory_space=pltpu.VMEM)
    anywhere = pl.BlockSpec(memory_space=pl.ANY)
    sem = pltpu.SemaphoreType.DMA
    sums, prob = pl.pallas_call(
        kernel,
        out_shape=(
            jax.ShapeDtypeStruct((16, 2048), F32),
            jax.ShapeDtypeStruct((1, IMG), F32),
        ),
        in_specs=[anywhere, anywhere] + [vmem] * 6,
        out_specs=(vmem, vmem),
        scratch_shapes=[
            pltpu.VMEM((2, 2, 4, 4, 2, 2, 16, WX), BF16),
            pltpu.VMEM((2, 2, 4, 2, 4, 2, 16, WY), BF16),
            pltpu.VMEM((2, 2, 4, 2, 2, 4, 16, WZ), BF16),
            pltpu.VMEM((2, 2, 4, 16, 128), BF16),
            pltpu.VMEM((2, 4, 4, 2, 2, 16, WX), BF16),
            pltpu.VMEM((2, 4, 2, 4, 2, 16, WY), BF16),
            pltpu.VMEM((2, 4, 2, 2, 4, 16, WZ), BF16),
            pltpu.VMEM((32, 512, IMG), BF16),
            pltpu.VMEM((16384, 128), F32),
            pltpu.VMEM((16, 2, 256, IMG), BF16),
            pltpu.VMEM((512, 128), F32),
            pltpu.VMEM((2, IMG, 16, 2 * A), BF16),
            pltpu.VMEM((2, 16, DEPTH, 2 * A), BF16),
            pltpu.VMEM((16, IMG, 2 * A), BF16),
            pltpu.VMEM((IMG, DEPTH), BF16),
            pltpu.VMEM((IMG, A), F32),
            pltpu.VMEM((R, IMG), F32),
            pltpu.VMEM((2, 2, 4, 2, 16, WX), BF16),
            pltpu.VMEM((2, 8, 2, 16, WZ), BF16),
            pltpu.VMEM((2, 2, 2, 4, 2, 16, WX), BF16),
            pltpu.VMEM((3, 2, 2, 4, 2, 16, WY), BF16),
            pltpu.VMEM((2, 2, 4, 4, 16, WZ), BF16),
            pltpu.VMEM((3, 2, 2, 2, 16, WX), BF16),
            pltpu.VMEM((3, 2, 4, 16, WY), BF16),
            pltpu.VMEM((3, 2, 4, 16, WZ), BF16),
            pltpu.VMEM((3, 2, 16, WX), BF16),
            pltpu.VMEM((3, 2, 16, WY), BF16),
            pltpu.VMEM((3, 2, 16, WZ), BF16),
            sem((4,)),
            sem((2, 40)),
            sem((2, 40)),
            sem((3, 8)),
            sem((3, 8)),
            sem((2, 2)),
            sem((2, 2)),
            sem((2, 8)),
            sem((2, 8)),
            sem((2, 2)),
            sem((2, 2)),
            sem((3, 8)),
            sem((3, 8)),
            sem((2, 8)),
            sem((2, 8)),
            sem((2, 3, 2, 3)),
            sem((2, 3, 2, 3)),
        ],
        compiler_params=pltpu.CompilerParams(
            collective_id=0, has_side_effects=True, vmem_limit_bytes=60 << 20
        ),
        cost_estimate=pl.CostEstimate(
            flops=14 << 30, bytes_accessed=24 << 20, transcendentals=1 << 20
        ),
        name="classify",
    )(
        spectra,
        jnp.asarray(shift_table()),
        offsets.T,
        groups.reshape(1, -1),
        ctf,
        noise_weight.reshape(1, -1),
        references,
        jnp.asarray(harmonic_rows()),
    )
    sums, prob = pl.pallas_call(
        write,
        out_shape=(
            jax.ShapeDtypeStruct((16, 2048), F32),
            jax.ShapeDtypeStruct((1, IMG), F32),
        ),
        in_specs=[vmem, vmem],
        out_specs=(vmem, vmem),
        name="write",
    )(sums, prob)
    return sums, prob.reshape(-1)


def solution(mesh):
    placed = (
        P(("img", "cls"), None, None),
        P(("img", "cls"), None),
        P(("img", "cls")),
        P(),
        P(),
        P("cls", None),
    )
    return jax.shard_map(
        on_device,
        mesh=mesh,
        in_specs=placed,
        out_specs=(P("cls", "img"), P(("img", "cls"))),
        check_vma=False,
    )
```
